32 devices in a mesh: cls: 4 (over y, x), dom: 8 (over z, core).
Axes of the slice: x: 2, y: 2, z: 4, core: 2. Of those that a mesh axis runs over, the one named last changes fastest.
Arguments:
- particles: bfloat16 [8192, 4096], P('dom', 'cls'), may hold values from -6 to 8
- candidates: int32 [8192, 2], P('dom'), may hold values from 0 to 7, all different within a row; in each aligned block of 1024 rows (0 to 1023, 1024 to 2047, ...) at most 512 rows name the same one
- defocus: int32 [8192], P('dom'), may hold values from 0 to 31
- ctf_table: float32 [32, 4096], P(None, 'cls'), may hold values from -1 to 1
- references: bfloat16 [32, 4096], P('dom', 'cls'), may hold values from -5 to 5
- rotations: bfloat16 [64, 64, 64], replicated, may hold values from -0.4 to 1.1
Outputs:
- class_sums: bfloat16 [32, 4096], P('dom', 'cls')
- class_weights: float32 [32, 4096], P('dom', 'cls')
- log_evidence: float32 [8192], P('dom')
The draws below stay inside these ranges and needn't reach their ends.
Inputs may be any that keep to these rules, and one draw needn't show every extreme that they name: The two candidates of a particle differ; among the 1024 particles of one index of dom no group is named by more than 512 entries, a bound that some block reaches.
All inputs are finite; a program needn't handle non-finite values.
Results may differ from the reference program's by a relative error of at most 0.0054.
Values may be sent and summed in bfloat16 or wider, within the bound.
No kernel may reach another device: no remote copies, remote signals or barrier semaphores. Data moves between devices by JAX's collectives and lax.ppermute only.
A program may use at most 128 MiB of HBM per device.

```python
import math
import jax
import jax.numpy as jnp
import numpy as np
from jax import lax

CYCLES = 64
ANG = 64
ROT = 64
CPG = 4
DEF = 32
TOK_DEV = 1024
PIX = 4096
CLASSES = 32
PARTS_SIZE = 8192
CAP = 512
N_DOM = 8


def draw_particles(key, part):
    noise_key = jax.random.fold_in(key, 11)
    values = jnp.clip(jax.random.normal(noise_key, (PARTS_SIZE, PIX), jnp.float32), -6.0, 6.0)
    return values.astype(jnp.bfloat16)


def draw_references(key, part):
    noise_key = jax.random.fold_in(key, 21)
    values = jnp.clip(jax.random.normal(noise_key, (CLASSES, PIX), jnp.float32), -5.0, 5.0)
    return values.astype(jnp.bfloat16)


def draw_ctf_table(key, part):
    noise_key = jax.random.fold_in(key, 31)
    values = jax.random.uniform(noise_key, (DEF, PIX), jnp.float32, -1.0, 1.0)
    return values


def draw_rotations(key, part):
    noise_key = jax.random.fold_in(key, 41)
    turn_ids = lax.broadcasted_iota(jnp.int32, (ROT, ANG, ANG), 0)
    target = lax.broadcasted_iota(jnp.int32, (ROT, ANG, ANG), 1)
    source = lax.broadcasted_iota(jnp.int32, (ROT, ANG, ANG), 2)
    offset = turn_ids * ANG // ROT
    hit = ((target - offset - source) % ANG == 0).astype(jnp.float32)
    noise = jnp.clip(jax.random.normal(noise_key, (ROT, ANG, ANG), jnp.float32), -4.0, 4.0)
    values = 0.7 * hit + noise * (0.35 / ANG ** 0.5)
    return values.astype(jnp.bfloat16)


def touch_ends(values, stream_key, smallest, high):
    dims = values.shape
    index_at = [jax.random.randint(jax.random.fold_in(stream_key, axis), (), 0, dims[axis]) for axis in range(len(dims))]
    values = values.at[tuple(index_at)].set(smallest)
    longest = dims.index(max(dims))
    index_at[longest] = (index_at[longest] + 1) % dims[longest]
    return values.at[tuple(index_at)].set(high)


def deal_out(rng, own, number, rows, number_of, top, limit, skew):
    sequence = jax.random.permutation(rng, number_of)
    heavy_load, usual = load_shares(number_of, rows * top, limit, skew, True), load_shares(number_of, rows * top, limit, skew, False)
    places = jnp.arange(number_of)

    def named(tallies, rotation):
        used = int((tallies > 0).sum())
        fixed = max(1, used // 4)
        moved = fixed + (places - fixed + rotation * (used - fixed)) % max(1, number_of - fixed)
        return jnp.zeros((number_of,), jnp.int32).at[sequence[jnp.where(places < fixed, places, moved)]].set(jnp.asarray(tallies, jnp.int32))

    tallies = jnp.where(number % 4 == 0, named(heavy_load, number // 4), named(usual, number - number // 4 - 1))
    mixed = jax.random.permutation(jax.random.fold_in(own, 3), number_of)
    giver, sink = mixed[0:number_of // 2 * 2:2], mixed[1:number_of // 2 * 2:2]
    margin = jnp.minimum(tallies[giver] - 1, limit - tallies[sink]) // 2
    margin = jnp.where((giver == sequence[0]) | (sink == sequence[0]) | (tallies[sink] == 0), 0, jnp.maximum(margin, 0))
    moved = jax.random.randint(jax.random.fold_in(own, 4), (number_of // 2,), 0, 1 << 20) % (margin + 1)
    tallies = tallies.at[giver].add(-moved).at[sink].add(moved)
    labels = jnp.searchsorted(jnp.cumsum(tallies), jnp.arange(rows * top), side="right").astype(jnp.int32)
    grid = labels.reshape(top, rows).T
    grid = grid[jax.random.permutation(jax.random.fold_in(own, 1), rows)]
    rotation = jax.random.randint(jax.random.fold_in(own, 2), (rows, 1), 0, top)
    return jnp.take_along_axis(grid, (jnp.arange(top)[None, :] + rotation) % top, axis=1)


def load_shares(number_of, total, limit, skew, full):
    loads = [(1 << 20) // math.isqrt(rank ** skew) + 1 for rank in range(1, number_of + 1)]
    largest = limit if full else min(limit, max(-(-total // number_of), total * loads[0] // sum(loads)))
    least = 1 if total - largest >= number_of - 1 else 0
    holding, rest = [largest] + [least] * (number_of - 1), total - largest - least * (number_of - 1)
    while rest > 0:
        free = [i for i in range(1, number_of) if holding[i] < largest] or [i for i in range(1, number_of) if holding[i] < limit]
        whole, remaining = sum([loads[i] for i in free]), rest
        for i in free:
            more = min(limit - holding[i], max(1, remaining * loads[i] // whole), rest)
            holding[i] = holding[i] + more
            rest = rest - more
    return np.array(holding)


def setup_inputs(seed: int = 0) -> dict:
    key_of = jax.random.split(jax.random.key(seed), 7)
    particles = draw_particles(jax.random.fold_in(key_of[6], 71), 0)
    candidates_keys = jax.random.split(jax.random.fold_in(key_of[1], 1), PARTS_SIZE // TOK_DEV)
    candidates_turns = jax.random.permutation(jax.random.fold_in(key_of[1], 3), PARTS_SIZE // TOK_DEV)
    candidates = jax.vmap(lambda own, number: deal_out(jax.random.fold_in(key_of[1], 2), own, number, TOK_DEV, N_DOM, 2, CAP, 2))(candidates_keys, candidates_turns).reshape((PARTS_SIZE, 2))
    defocus = touch_ends(jax.random.randint(key_of[2], (PARTS_SIZE,), 0, DEF), jax.random.fold_in(key_of[2], 1), 0, DEF - 1).astype(jnp.int32)
    ctf_table = draw_ctf_table(jax.random.fold_in(key_of[6], 71), 0)
    references = draw_references(jax.random.fold_in(key_of[6], 71), 0)
    rotations = draw_rotations(jax.random.fold_in(key_of[6], 71), 0)
    return {"particles": particles, "candidates": candidates, "defocus": defocus, "ctf_table": ctf_table, "references": references, "rotations": rotations}


highest = lax.Precision.HIGHEST


def slot_layout(candidates):
    entries = candidates.reshape(N_DOM, 2 * TOK_DEV).astype(jnp.int32)
    owner_ids = jnp.arange(N_DOM, dtype=jnp.int32)
    onehot_owner = (entries[:, :, None] == owner_ids[None, None, :]).astype(jnp.int32)
    entry_rank = jnp.cumsum(onehot_owner, axis=1) - onehot_owner
    slot_of = jnp.sum(entry_rank * onehot_owner, axis=2).astype(jnp.int32)
    return entries, slot_of


def reference(particles, candidates, defocus, ctf_table, references, rotations):
    entries, slot_of = slot_layout(candidates)
    source_ids = jnp.broadcast_to(jnp.arange(N_DOM, dtype=jnp.int32)[:, None], entries.shape)
    entry_ids = jnp.broadcast_to(jnp.arange(2 * TOK_DEV, dtype=jnp.int32)[None, :], entries.shape)
    slot_entry = jnp.full((N_DOM, N_DOM, CAP), -1, jnp.int32).at[entries, source_ids, slot_of].set(entry_ids)
    slot_total = N_DOM * CAP
    live_flat = (slot_entry >= 0).reshape(N_DOM, slot_total)
    src_rows = (jnp.arange(N_DOM, dtype=jnp.int32)[None, :, None] * TOK_DEV + jnp.maximum(slot_entry, 0) // 2).astype(jnp.int32).reshape(N_DOM, slot_total)
    turn_maps = rotations.astype(jnp.float32)
    ref_grid = references.astype(jnp.float32).reshape(CLASSES, CYCLES, ANG)
    rotated = jnp.einsum("cla,rba->crlb", ref_grid, turn_maps, precision=highest).astype(jnp.bfloat16)
    rotated = rotated.reshape(N_DOM, CPG * ROT, PIX)
    ctf_power = ctf_table * ctf_table
    inverse_noise = 4.0 / (PIX ** 0.5)
    kind_ids = jnp.arange(DEF, dtype=jnp.int32)

    def prepare(owner_rows, owner_live):
        defocus_rows = jnp.where(owner_live, defocus[owner_rows], -1)
        picked = (defocus_rows[:, None] == kind_ids[None, :]).astype(jnp.float32)
        ctf_rows = jnp.dot(picked, ctf_table, precision=highest)
        weighted = (particles[owner_rows].astype(jnp.float32) * ctf_rows).astype(jnp.bfloat16)
        return picked, weighted

    def score_group(packed):
        owner_rows, owner_live, owner_refs = packed
        picked, weighted = prepare(owner_rows, owner_live)
        cross_term = jnp.dot(weighted, owner_refs.T, preferred_element_type=jnp.float32)
        square = owner_refs.astype(jnp.float32) ** 2
        energy = jnp.dot(ctf_power, square.T, precision=highest)
        energy_rows = jnp.dot(picked, energy, precision=highest)
        return inverse_noise * (cross_term - 0.5 * energy_rows)

    scores = lax.map(score_group, (src_rows, live_flat, rotated))
    slot_max = jnp.max(scores, axis=2)
    slot_sum = jnp.sum(jnp.exp(scores - slot_max[:, :, None]), axis=2)
    flat_slot = jnp.arange(N_DOM, dtype=jnp.int32)[:, None] * CAP + slot_of
    pair_max = slot_max[entries, flat_slot].reshape(PARTS_SIZE, 2)
    pair_sum = slot_sum[entries, flat_slot].reshape(PARTS_SIZE, 2)
    pair_best = jnp.max(pair_max, axis=1, keepdims=True)
    log_evidence = pair_best[:, 0] + jnp.log(jnp.sum(pair_sum * jnp.exp(pair_max - pair_best), axis=1))

    def accumulate(packed):
        owner_rows, owner_live, owner_scores = packed
        picked, weighted = prepare(owner_rows, owner_live)
        weights = jnp.where(owner_live[:, None], jnp.exp(owner_scores - log_evidence[owner_rows][:, None]), 0.0).astype(jnp.bfloat16)
        rot_sum = jnp.dot(weights.T, weighted, preferred_element_type=jnp.float32)
        pair_kind = jnp.dot(weights.astype(jnp.float32).T, picked, precision=highest)
        rot_weight = jnp.dot(pair_kind, ctf_power, precision=highest)
        back_sum = jnp.einsum("crlb,rba->cla", rot_sum.reshape(CPG, ROT, CYCLES, ANG), turn_maps, precision=highest)
        back_weight = jnp.einsum("crlb,rba->cla", rot_weight.reshape(CPG, ROT, CYCLES, ANG), turn_maps, precision=highest)
        return back_sum.reshape(CPG, PIX).astype(jnp.bfloat16), back_weight.reshape(CPG, PIX)

    class_sums, class_weights = lax.map(accumulate, (src_rows, live_flat, scores))
    return class_sums.reshape(CLASSES, PIX), class_weights.reshape(CLASSES, PIX), log_evidence
```

```python
import functools
import math

import jax
import jax.numpy as jnp
from jax import lax
from jax.experimental import pallas as pl
from jax.experimental.pallas import tpu as pltpu
from jax.sharding import PartitionSpec as P

f32, bf16 = jnp.float32, jnp.bfloat16
VMEM = pl.BlockSpec(memory_space=pltpu.VMEM)
SMEM = pl.BlockSpec(memory_space=pltpu.SMEM)
BLOCK = 32
NN = (((1,), (0,)), ((), ()))
NT = (((1,), (1,)), ((), ()))
TN = (((0,), (0,)), ((), ()))


def dot(a, b, dims):
    return lax.dot_general(a, b, dims, preferred_element_type=f32)


def split3(x):
    hi = x.astype(bf16)
    rest = x - hi.astype(f32)
    mid = rest.astype(bf16)
    return hi, mid, (rest - mid.astype(f32)).astype(bf16)


def one_hot(row, kinds, copies):
    ids = lax.broadcasted_iota(jnp.int32, (kinds, row.shape[1]), 0)
    hit = jnp.where(ids == row, 1.0, 0.0).astype(bf16)
    return jnp.concatenate([hit] * copies, axis=0)


def diagonal(turn2, angles, width):
    wide = jnp.concatenate([turn2] * (width // (2 * angles)), axis=1)
    tall = jnp.concatenate([wide] * (width // angles), axis=0)
    row = lax.broadcasted_iota(jnp.int32, (width, width), 0) // angles
    col = lax.broadcasted_iota(jnp.int32, (width, width), 1) // angles
    return jnp.where(row == col, tall, jnp.zeros((), bf16))


def weigh_kernel(pixels, kind, table, out):
    table3 = jnp.concatenate(split3(table[...]), axis=0)
    hit3 = one_hot(kind[...], table.shape[0], 3)
    rows = dot(hit3, table3, TN)
    out[...] = (pixels[...].astype(f32) * rows).astype(bf16)


def weigh(particles, kind, table):
    count, pixels = particles.shape
    rows = math.gcd(count, 256)
    return pl.pallas_call(
        weigh_kernel,
        grid=(count // rows,),
        in_specs=[
            pl.BlockSpec((rows, pixels), lambda i: (i, 0)),
            pl.BlockSpec((1, rows), lambda i: (0, i)),
            pl.BlockSpec(table.shape, lambda i: (0, 0)),
        ],
        out_specs=pl.BlockSpec((rows, pixels), lambda i: (i, 0)),
        out_shape=jax.ShapeDtypeStruct((count, pixels), bf16),
        compiler_params=pltpu.CompilerParams(vmem_limit_bytes=40 << 20),
        cost_estimate=pl.CostEstimate(
            flops=2 * count * pixels * 96, bytes_accessed=4 * count * pixels, transcendentals=0
        ),
        name="weigh",
    )(particles, kind, table)


def rotate_kernel(refs, turns, table, rotated, energy, mean, wide, center):
    classes, pixels = refs.shape
    turn_count, angles, _ = turns.shape
    width = min(256, pixels)
    quads = pixels // width
    lhs = jnp.concatenate([refs[:, q * width:(q + 1) * width] for q in range(quads)], axis=0)

    def turn(r, carry):
        matrix = diagonal(turns[r], angles, width)
        product = dot(lhs, matrix, NT)
        for q in range(quads):
            for t in range(width // 128):
                wide[q * (width // 128) + t, pl.ds(r, classes, stride=turn_count), :] = product[
                    q * classes:(q + 1) * classes, t * 128:(t + 1) * 128
                ]
        return carry

    lax.fori_loop(0, turn_count, turn, 0, unroll=4)
    power = table[...] * table[...]
    kinds = power.shape[0]
    power2 = jnp.concatenate(split3(power)[:2], axis=0)
    pairs = classes * turn_count
    rows = 256

    def part(i, carry):
        at = pl.ds(pl.multiple_of(i * rows, rows), rows)
        total = jnp.zeros((rows, 2 * kinds), f32)
        for t in range(pixels // 128):
            value = wide[t, at, :].astype(bf16)
            rotated[at, t * 128:(t + 1) * 128] = value
        for q in range(quads):
            value = rotated[at, q * width:(q + 1) * width].astype(f32)
            square = value * value
            hi = square.astype(bf16)
            lo = (square - hi.astype(f32)).astype(bf16)
            own = power2[:, q * width:(q + 1) * width]
            total = total + dot(hi, own, NT) + dot(lo, own, NT)
        total = -0.5 * (total[:, :kinds] + total[:, kinds:])
        energy[at, :] = total
        return carry + jnp.sum(total, axis=0, keepdims=True)

    summed = lax.fori_loop(0, pairs // rows, part, jnp.zeros((1, kinds), f32))

    @pl.when(pl.program_id(0) == 0)
    def _():
        center[...] = summed * (1.0 / pairs)

    mean[...] = center[...]


def rotate(refs, turns2, table):
    classes, pixels = refs.shape
    turn_count = turns2.shape[0]
    kinds = table.shape[0]
    block = min(BLOCK, classes)
    pairs = block * turn_count
    return pl.pallas_call(
        rotate_kernel,
        grid=(classes // block,),
        in_specs=[
            pl.BlockSpec((block, pixels), lambda i: (i, 0)),
            pl.BlockSpec(turns2.shape, lambda i: (0, 0, 0)),
            pl.BlockSpec(table.shape, lambda i: (0, 0)),
        ],
        out_specs=[
            pl.BlockSpec((pairs, pixels), lambda i: (i, 0)),
            pl.BlockSpec((pairs, kinds), lambda i: (i, 0)),
            pl.BlockSpec((1, kinds), lambda i: (0, 0)),
        ],
        out_shape=[
            jax.ShapeDtypeStruct((classes * turn_count, pixels), bf16),
            jax.ShapeDtypeStruct((classes * turn_count, kinds), f32),
            jax.ShapeDtypeStruct((1, kinds), f32),
        ],
        scratch_shapes=[
            pltpu.VMEM((pixels // 128, pairs, 128), f32),
            pltpu.VMEM((1, kinds), f32),
        ],
        compiler_params=pltpu.CompilerParams(vmem_limit_bytes=50 << 20),
        cost_estimate=pl.CostEstimate(
            flops=8 * classes * turn_count * pixels * 64,
            bytes_accessed=2 * classes * turn_count * pixels,
            transcendentals=0,
        ),
        name="rotate",
    )(refs, turns2, table)


def score_kernel(groups, scale, me, weighted, kind, names, rotated, energy, mean, own, *rest):
    others, acc = rest[:-1], rest[-1]
    step = pl.program_id(0)
    count = weighted.shape[0]
    kinds = energy.shape[1]
    pairs = rotated.shape[0] // groups
    span = min(256, count)
    for n in range(count // span):
        cols = pl.ds(n * span, span)
        hit3 = one_hot(kind[:, cols], kinds, 3)
        first, second = names[0:1, cols], names[1:2, cols]
        pix = weighted[cols, :]
        for g in range(groups):
            at = pl.ds(g * pairs, pairs)
            shift = jnp.concatenate(split3(energy[at, :] - mean[...]), axis=1)
            value = scale * (dot(rotated[at, :], pix, NT) + dot(shift, hit3, NN))
            group = step * groups + g
            for k, name in enumerate((first, second)):
                rows = pl.ds(k * pairs, pairs)
                if g == 0:
                    base = jnp.where(step == 0, jnp.zeros_like(value), acc[rows, cols])
                    acc[rows, cols] = jnp.where(name == group, value, base)
                else:
                    acc[rows, cols] = jnp.where(name == group, value, acc[rows, cols])

    @pl.when(step == pl.num_programs(0) - 1)
    def _():
        share = own.shape[1]
        for k, out in enumerate((own,) + others):
            start = pl.multiple_of((me[0] ^ k) * share, share)
            out[...] = acc[:, pl.ds(start, share)]


def score(weighted, kind, names, rotated, energy, mean, me, peers, group_pairs, scale):
    count, pixels = weighted.shape
    kinds = energy.shape[1]
    groups_all = rotated.shape[0] // group_pairs
    groups = math.gcd(groups_all, 8)
    share = count // peers
    rows = 2 * group_pairs
    out = pl.BlockSpec((rows, share), lambda i: (0, 0))
    return pl.pallas_call(
        functools.partial(score_kernel, groups, scale),
        grid=(groups_all // groups,),
        in_specs=[
            SMEM,
            pl.BlockSpec((count, pixels), lambda i: (0, 0)),
            pl.BlockSpec((1, count), lambda i: (0, 0)),
            pl.BlockSpec((2, count), lambda i: (0, 0)),
            pl.BlockSpec((groups * group_pairs, pixels), lambda i: (i, 0)),
            pl.BlockSpec((groups * group_pairs, kinds), lambda i: (i, 0)),
            pl.BlockSpec((1, kinds), lambda i: (0, 0)),
        ],
        out_specs=[out] * peers,
        out_shape=[jax.ShapeDtypeStruct((rows, share), f32)] * peers,
        scratch_shapes=[pltpu.VMEM((rows, count), f32)],
        compiler_params=pltpu.CompilerParams(vmem_limit_bytes=50 << 20),
        cost_estimate=pl.CostEstimate(
            flops=2 * rotated.shape[0] * pixels * count,
            bytes_accessed=2 * rotated.shape[0] * pixels,
            transcendentals=0,
        ),
        name="score",
    )(me, weighted, kind, names, rotated, energy, mean)


def soften_kernel(scores, mean, out):
    value = scores[...]
    rows, share = value.shape
    top = jnp.max(value, axis=0, keepdims=True)
    grown = jnp.exp(value - top)
    total = jnp.sum(grown, axis=0, keepdims=True)
    out[:rows, :] = (grown * (1.0 / total)).astype(bf16)
    kinds = mean.shape[1]
    centers = mean[...]
    if kinds < share:
        centers = jnp.concatenate([centers, jnp.zeros((1, share - kinds), f32)], axis=1)
    tail = jnp.zeros((16, share), f32)
    at = lax.broadcasted_iota(jnp.int32, tail.shape, 0)
    for i, row in enumerate(split3(top + jnp.log(total)) + split3(centers)):
        tail = jnp.where(at == i, row.astype(f32), tail)
    out[rows:, :] = tail.astype(bf16)


def soften(scores, mean):
    rows, share = scores.shape
    return pl.pallas_call(
        soften_kernel,
        in_specs=[VMEM, VMEM],
        out_specs=VMEM,
        out_shape=jax.ShapeDtypeStruct((rows + 16, share), bf16),
        cost_estimate=pl.CostEstimate(
            flops=4 * rows * share, bytes_accessed=6 * rows * share, transcendentals=rows * share
        ),
        name="soften",
    )(scores, mean)


def collect_kernel(groups, scale, peers, chunks, me, kind, names, weighted, turns, table, *rest):
    blocks = rest[:peers * chunks]
    sums, logs, weights, rot_sum, rot_weight = rest[peers * chunks:]
    step = pl.program_id(0)
    count, pixels = weighted.shape
    kinds = table.shape[0]
    turn_count, angles, _ = turns.shape
    share = blocks[0].shape[1]
    rows = weights.shape[0]
    pairs = rows // 2
    classes = groups * pairs // turn_count
    tiles = pixels // 128

    @pl.when(step == 0)
    def _():
        center = jnp.zeros((1, share), f32)
        for k in range(peers):
            for c in range(chunks):
                block = blocks[c * peers + k]
                start = pl.multiple_of((c * peers + (me[0] ^ k)) * share, share)
                weights[:, pl.ds(start, share)] = block[:rows, :]
                tail = block[rows:, :].astype(f32)
                logs[0:1, pl.ds(start, share)] = tail[0:1] + tail[1:2] + tail[2:3]
                if c == 0:
                    center = center + (tail[3:4] + tail[4:5] + tail[5:6])
        center3 = jnp.concatenate([part.astype(f32) for part in split3(center[:, :kinds])], axis=0)
        center3 = jnp.concatenate([center3, jnp.zeros((13, kinds), f32)], axis=0).astype(bf16)
        moved = dot(center3, one_hot(kind[...], kinds, 1), NN)
        logs[...] = logs[...] + scale * jnp.sum(moved, axis=0, keepdims=True)

    hit = one_hot(kind[...], kinds, 1)
    power = table[...] * table[...]
    power3 = jnp.concatenate(split3(power)[:2], axis=0)
    first, second = names[0:1, :], names[1:2, :]
    zero = jnp.zeros((), bf16)
    for g in range(groups):
        group = step * groups + g
        dense = jnp.where(first == group, weights[:pairs, :], zero) + jnp.where(
            second == group, weights[pairs:, :], zero
        )
        at = pl.ds(g * pairs, pairs)
        by_kind = dot(dense, hit, NT)
        hi = by_kind.astype(bf16)
        lo = (by_kind - hi.astype(f32)).astype(bf16)
        value = dot(dense, weighted[...], NN)
        for t in range(tiles):
            rot_sum[t, at, :] = value[:, t * 128:(t + 1) * 128]
        value = dot(jnp.concatenate([hi, hi], axis=1), power3, NN) + dot(lo, power3[:kinds], NN)
        for t in range(tiles):
            rot_weight[t, at, :] = value[:, t * 128:(t + 1) * 128]

    width = min(256, pixels)
    quads = pixels // width
    per = width // 128

    def turn(r, carry):
        matrix = diagonal(turns[r], angles, width)
        at = pl.ds(r, classes, stride=turn_count)
        parts = []
        for source in (rot_sum, rot_weight):
            for q in range(quads):
                parts.append(jnp.concatenate([source[q * per + t, at, :] for t in range(per)], axis=1))
        lhs = jnp.concatenate(parts, axis=0)
        hi = lhs.astype(bf16)
        lo = (lhs - hi.astype(f32)).astype(bf16)
        return carry + dot(hi, matrix, NN) + dot(lo, matrix, NN)

    total = lax.fori_loop(0, turn_count, turn, jnp.zeros((2 * quads * classes, width), f32), unroll=2)
    for q in range(2 * quads):
        sums[:, q * width:(q + 1) * width] = total[q * classes:(q + 1) * classes, :]


def collect(blocks, chunks, kind, names, weighted, turns2, table, me, group_pairs, groups_all, scale):
    count, pixels = weighted.shape
    turn_count = turns2.shape[0]
    peers = len(blocks) // chunks
    groups = math.gcd(groups_all, 8)
    classes = groups * group_pairs // turn_count
    whole = lambda a: pl.BlockSpec(a.shape, lambda i: (0,) * a.ndim)
    return pl.pallas_call(
        functools.partial(collect_kernel, groups, scale, peers, chunks),
        grid=(groups_all // groups,),
        in_specs=[SMEM] + [whole(a) for a in (kind, names, weighted, turns2, table)] + [whole(b) for b in blocks],
        out_specs=[
            pl.BlockSpec((classes, 2 * pixels), lambda i: (i, 0)),
            pl.BlockSpec((1, count), lambda i: (0, 0)),
        ],
        out_shape=[
            jax.ShapeDtypeStruct((groups_all * group_pairs // turn_count, 2 * pixels), f32),
            jax.ShapeDtypeStruct((1, count), f32),
        ],
        scratch_shapes=[
            pltpu.VMEM((2 * group_pairs, count), bf16),
            pltpu.VMEM((pixels // 128, groups * group_pairs, 128), f32),
            pltpu.VMEM((pixels // 128, groups * group_pairs, 128), f32),
        ],
        compiler_params=pltpu.CompilerParams(vmem_limit_bytes=56 << 20),
        cost_estimate=pl.CostEstimate(
            flops=4 * groups_all * group_pairs * pixels * count,
            bytes_accessed=4 * count * pixels,
            transcendentals=0,
        ),
        name="collect",
    )(me, kind, names, weighted, turns2, table, *blocks)


def swap(x, axis, k):
    return lax.ppermute(x, axis, [(i, i ^ k) for i in range(lax.axis_size(axis))])


def gather_dom(x):
    size = lax.axis_size("dom")
    if size & (size - 1) or size > 8:
        return lax.all_gather(x, "dom", axis=0, tiled=True)
    here = lax.axis_index("dom")
    out = jnp.zeros((size,) + x.shape, x.dtype)
    for k in range(size):
        out = lax.dynamic_update_index_in_dim(out, swap(x, "dom", k) if k else x, here ^ k, 0)
    return out.reshape((size * x.shape[0],) + x.shape[1:])


def scatter_dom(x):
    size = lax.axis_size("dom")
    if size & (size - 1) or size > 8:
        return lax.psum_scatter(x, "dom", scatter_dimension=0, tiled=True)
    here = lax.axis_index("dom")
    x = x.reshape((size, x.shape[0] // size) + x.shape[1:])
    pick = lambda k: lax.dynamic_index_in_dim(x, here ^ k, 0, keepdims=False)
    total = pick(0)
    for k in range(1, size):
        total = total + swap(pick(k), "dom", k)
    return total


def local(particles, candidates, defocus, ctf_table, references, rotations):
    count, pixels = particles.shape
    peers = lax.axis_size("cls")
    turn_count = rotations.shape[0]
    group_pairs = references.shape[0] * turn_count
    groups = lax.axis_size("dom")
    scale = 4.0 / math.sqrt(pixels * peers)
    me = lax.axis_index("cls").astype(jnp.int32).reshape(1)
    kind = defocus.reshape(1, count)
    names = candidates.T
    turns2 = jnp.concatenate([rotations, rotations], axis=2)
    all_refs = gather_dom(references)
    weighted = weigh(particles, kind, ctf_table)
    rotated, energy, mean = rotate(all_refs, turns2, ctf_table)
    chunks = 2
    size = count // chunks
    blocks = []
    for c in range(chunks):
        at = slice(c * size, (c + 1) * size)
        cut = score(
            weighted[at], kind[:, at], names[:, at], rotated, energy, mean, me, peers, group_pairs, scale
        )
        total = cut[0]
        for k in range(1, peers):
            total = total + swap(cut[k].astype(jnp.float16), "cls", k).astype(f32)
        own = soften(total, mean)
        blocks.extend([own] + [swap(own, "cls", k) for k in range(1, peers)])
    sums, logs = collect(
        blocks, chunks, kind, names, weighted, turns2, ctf_table, me, group_pairs, groups, scale
    )
    total = scatter_dom(sums)
    return total[:, :pixels].astype(bf16), total[:, pixels:], logs.reshape(count)


def solution(mesh):
    in_specs = (P("dom", "cls"), P("dom", None), P("dom"), P(None, "cls"), P("dom", "cls"), P())
    out_specs = (P("dom", "cls"), P("dom", "cls"), P("dom"))
    return jax.shard_map(local, mesh=mesh, in_specs=in_specs, out_specs=out_specs, check_vma=False)
```

```python
import functools
import math

import jax
import jax.numpy as jnp
from jax import lax
from jax.experimental import pallas as pl
from jax.experimental.pallas import tpu as pltpu
from jax.sharding import PartitionSpec as P

f32, bf16 = jnp.float32, jnp.bfloat16
VMEM = pl.BlockSpec(memory_space=pltpu.VMEM)
SMEM = pl.BlockSpec(memory_space=pltpu.SMEM)
LANES, ROWS = 128, 8
NN = (((1,), (0,)), ((), ()))
NT = (((1,), (1,)), ((), ()))


def dot(a, b, dims):
    return lax.dot_general(a, b, dims, preferred_element_type=f32)


def split(x, parts):
    out = []
    for _ in range(parts):
        out.append(x.astype(bf16))
        x = x - out[-1].astype(f32)
    return out


def limits(mib, flops, moved, transcendentals=0):
    return dict(
        compiler_params=pltpu.CompilerParams(vmem_limit_bytes=mib << 20),
        cost_estimate=pl.CostEstimate(flops=flops, bytes_accessed=moved, transcendentals=transcendentals),
    )


def block_spec(steps, shape, dim):
    if steps == 1:
        return VMEM
    index = lambda i: tuple(i if d == dim else 0 for d in range(len(shape)))
    return pl.BlockSpec(shape, index)


def same_spec(steps, shape):
    return VMEM if steps == 1 else pl.BlockSpec(shape, lambda i: (0,) * len(shape))


def prepare_kernel(turns, table, matrix, response):
    turn_count, angles, _ = turns.shape
    kinds, pixels = table.shape
    per = LANES // angles
    pack = matrix.shape[1] // LANES
    tiles = pixels // LANES
    row = lax.broadcasted_iota(jnp.int32, (LANES, LANES), 0) // angles
    col = lax.broadcasted_iota(jnp.int32, (LANES, LANES), 1) // angles
    zero = jnp.zeros((), bf16)
    power = table[...] * table[...]
    hi, lo = split(power, 2)
    lhs = jnp.concatenate(
        [
            jnp.concatenate([part[:, t * LANES:(t + 1) * LANES] for part in (hi, lo)], axis=1)
            for t in range(tiles)
        ],
        axis=0,
    )
    for i in range(turn_count // pack):
        wide = []
        for j in range(pack):
            turn = turns[i * pack + j]
            turn = jnp.concatenate([jnp.concatenate([turn] * per, axis=1)] * per, axis=0)
            wide.append(jnp.where(row == col, turn, zero))
        wide = jnp.concatenate(wide, axis=1)
        matrix[i * LANES:(i + 1) * LANES, :] = wide
        value = dot(lhs, jnp.concatenate([wide, wide], axis=0), NN).astype(bf16)
        for j in range(pack):
            for t in range(tiles):
                response[i * kinds:(i + 1) * kinds, j * pixels + t * LANES:j * pixels + (t + 1) * LANES] = value[
                    t * kinds:(t + 1) * kinds, j * LANES:(j + 1) * LANES
                ]


def prepare(turns, table, pack):
    turn_count, angles, _ = turns.shape
    kinds, pixels = table.shape
    steps = turn_count // pack
    return pl.pallas_call(
        prepare_kernel,
        in_specs=[VMEM, VMEM],
        out_specs=[VMEM, VMEM],
        out_shape=[
            jax.ShapeDtypeStruct((steps * LANES, pack * LANES), bf16),
            jax.ShapeDtypeStruct((steps * kinds, pack * pixels), bf16),
        ],
        name="prepare",
        **limits(24, 4 * steps * kinds * pack * pixels * LANES, 2 * steps * kinds * pack * pixels),
    )(turns, table)


def weigh_kernel(pixels, kind, table, out):
    kinds, width = table.shape
    table3 = jnp.concatenate(split(table[...], 3), axis=0)
    ids = lax.broadcasted_iota(jnp.int32, (LANES, kind.shape[1]), 0)
    hit = jnp.where((ids % kinds == kind[...]) & (ids < 3 * kinds), 1.0, 0.0)
    hit = hit.T.astype(bf16)
    rows = dot(hit[:, :3 * kinds], table3, NN)
    out[:, :width] = (pixels[...].astype(f32) * rows).astype(bf16)
    out[:, width:] = hit


def weigh(particles, kind, table):
    count, pixels = particles.shape
    rows = math.gcd(count, 256)
    return pl.pallas_call(
        weigh_kernel,
        grid=(count // rows,),
        in_specs=[
            pl.BlockSpec((rows, pixels), lambda i: (i, 0)),
            pl.BlockSpec((1, rows), lambda i: (0, i)),
            pl.BlockSpec(table.shape, lambda i: (0, 0)),
        ],
        out_specs=pl.BlockSpec((rows, pixels + LANES), lambda i: (i, 0)),
        out_shape=jax.ShapeDtypeStruct((count, pixels + LANES), bf16),
        name="weigh",
        **limits(16, 2 * count * pixels * 96, 4 * count * pixels),
    )(particles, kind, table)


def rotate_kernel(groups, turn_count, refs, matrix, table, rotated, mean, center, energy):
    kinds, pixels = table.shape
    pack = matrix.shape[1] // LANES
    cpg = ROWS // pack
    tiles = pixels // LANES
    group_pairs = cpg * turn_count
    source = refs[...].astype(f32)
    inside = lax.broadcasted_iota(jnp.int32, (groups * ROWS, LANES), 0) % ROWS // cpg
    lhs = jnp.concatenate(
        [
            jnp.concatenate(
                [jnp.where(inside == j, source[:, t * LANES:(t + 1) * LANES], 0.0) for j in range(pack)], axis=1
            )
            for t in range(tiles)
        ],
        axis=0,
    ).astype(bf16)
    for s in range(turn_count // (2 * pack)):
        value = dot(lhs, matrix[s * 2 * LANES:(s + 1) * 2 * LANES, :], NT)
        for t in range(tiles):
            for g in range(groups):
                at = (t * groups + g) * ROWS
                pair = [value[at:at + ROWS, h * LANES:(h + 1) * LANES] for h in range(2)]
                to = g * group_pairs + s * 2 * ROWS
                rotated[to:to + 2 * ROWS, t * LANES:(t + 1) * LANES] = jnp.concatenate(pair, axis=0).astype(bf16)
    power = table[...] * table[...]
    power2 = jnp.concatenate(split(power, 2), axis=0)
    pairs = groups * group_pairs
    rows = math.gcd(pairs, 256)
    summed = jnp.zeros((kinds, 1), f32)
    for i in range(pairs // rows):
        at = slice(i * rows, (i + 1) * rows)
        value = rotated[at, :pixels].astype(f32)
        hi, lo = split(value * value, 2)
        total = dot(power2, hi, NT) + dot(power2, lo, NT)
        total = -0.5 * (total[:kinds] + total[kinds:])
        energy[:, at] = total
        summed = summed + jnp.sum(total, axis=1, keepdims=True)

    @pl.when(pl.program_id(0) == 0)
    def _():
        center[...] = summed * (1.0 / pairs)

    spread = lax.broadcasted_iota(jnp.int32, (kinds, LANES), 0) == lax.broadcasted_iota(jnp.int32, (kinds, LANES), 1)
    mean[...] = jnp.sum(jnp.where(spread, center[...], 0.0), axis=0, keepdims=True)
    blank = jnp.zeros((LANES - 3 * kinds, LANES), f32)
    for i in range(pairs // LANES):
        at = slice(i * LANES, (i + 1) * LANES)
        parts = [part.astype(f32) for part in split(energy[:, at] - center[...], 3)]
        rotated[at, pixels:] = jnp.concatenate(parts + [blank], axis=0).T.astype(bf16)


def rotate(refs, matrix, table, turn_count, groups):
    kinds, pixels = table.shape
    groups_all = refs.shape[0] // ROWS
    steps = groups_all // groups
    cpg = ROWS * LANES // matrix.shape[1]
    pairs = groups * cpg * turn_count
    return pl.pallas_call(
        functools.partial(rotate_kernel, groups, turn_count),
        grid=(steps,),
        in_specs=[
            block_spec(steps, (groups * ROWS, pixels), 0),
            same_spec(steps, matrix.shape),
            same_spec(steps, table.shape),
        ],
        out_specs=[block_spec(steps, (pairs, pixels + LANES), 0), same_spec(steps, (1, LANES))],
        out_shape=[
            jax.ShapeDtypeStruct((steps * pairs, pixels + LANES), bf16),
            jax.ShapeDtypeStruct((1, LANES), f32),
        ],
        scratch_shapes=[pltpu.VMEM((kinds, 1), f32), pltpu.VMEM((kinds, pairs), f32)],
        name="rotate",
        **limits(24, 8 * steps * pairs * pixels * 64, 2 * steps * pairs * pixels),
    )(refs, matrix, table)


def score_kernel(groups, scale, me, weighted, names, rotated, *rest):
    outs, acc = rest[:-1], rest[-1]
    step = pl.program_id(0)
    count = weighted.shape[0]
    pairs = rotated.shape[0] // groups
    span = math.gcd(count, 256)
    for n in range(count // span):
        cols = slice(n * span, (n + 1) * span)
        pix = weighted[cols, :]
        for g in range(groups):
            value = scale * dot(rotated[g * pairs:(g + 1) * pairs, :], pix, NT)
            group = step * groups + g
            for k in range(2):
                rows = slice(k * pairs, (k + 1) * pairs)
                hit = names[k:k + 1, cols] == group
                if g == 0:
                    hit = hit | (step == 0)
                acc[rows, cols] = jnp.where(hit, value, acc[rows, cols])

    @pl.when(step == pl.num_programs(0) - 1)
    def _():
        share = outs[0].shape[1]
        for k, out in enumerate(outs):
            start = pl.multiple_of((me[0] ^ k) * share, share)
            out[...] = acc[:, pl.ds(start, share)]


def score(weighted, names, rotated, me, peers, group_pairs, groups, scale):
    count, width = weighted.shape
    steps = rotated.shape[0] // (group_pairs * groups)
    share = count // peers
    rows = 2 * group_pairs
    return pl.pallas_call(
        functools.partial(score_kernel, groups, scale),
        grid=(steps,),
        in_specs=[
            SMEM,
            same_spec(steps, weighted.shape),
            same_spec(steps, names.shape),
            block_spec(steps, (groups * group_pairs, width), 0),
        ],
        out_specs=[same_spec(steps, (rows, share))] * peers,
        out_shape=[jax.ShapeDtypeStruct((rows, share), f32)] * peers,
        scratch_shapes=[pltpu.VMEM((rows, count), f32)],
        name="score",
        **limits(24, 2 * rotated.shape[0] * width * count, 2 * rotated.shape[0] * width),
    )(me, weighted, names, rotated)


def soften_kernel(scores, mean, out):
    value = scores[...]
    rows, share = value.shape
    top = jnp.max(value, axis=0, keepdims=True)
    grown = jnp.exp(value - top)
    total = jnp.sum(grown, axis=0, keepdims=True)
    out[:rows, :] = (grown * (1.0 / total)).astype(bf16)
    tail = jnp.zeros((2 * ROWS, share), f32)
    at = lax.broadcasted_iota(jnp.int32, tail.shape, 0)
    centers = mean[...]
    if share > LANES:
        centers = jnp.concatenate([centers, jnp.zeros((1, share - LANES), f32)], axis=1)
    for i, row in enumerate(split(top + jnp.log(total), 3) + split(centers, 3)):
        tail = jnp.where(at == i, row.astype(f32), tail)
    out[rows:, :] = tail.astype(bf16)


def soften(scores, mean):
    rows, share = scores.shape
    return pl.pallas_call(
        soften_kernel,
        in_specs=[VMEM, VMEM],
        out_specs=VMEM,
        out_shape=jax.ShapeDtypeStruct((rows + 2 * ROWS, share), bf16),
        name="soften",
        **limits(8, 4 * rows * share, 6 * rows * share, rows * share),
    )(scores, mean)


def collect_kernel(groups, turn_count, kinds, scale, peers, chunks, me, names, weighted, matrix, response, *rest):
    blocks = rest[:peers * chunks]
    sums, logs, weights, lhs, by_kind = rest[peers * chunks:]
    step = pl.program_id(0)
    count, pixels = weighted.shape[0], weighted.shape[1] - LANES
    share = blocks[0].shape[1]
    rows = weights.shape[0]
    pairs = rows // 2
    pack = matrix.shape[1] // LANES
    cpg = ROWS // pack
    tiles = pixels // LANES
    turns = turn_count // pack

    @pl.when(step == 0)
    def _():
        center = jnp.zeros((1, share), f32)
        for k in range(peers):
            for c in range(chunks):
                block = blocks[c * peers + k]
                start = pl.multiple_of((c * peers + (me[0] ^ k)) * share, share)
                weights[:, pl.ds(start, share)] = block[:rows, :]
                tail = block[rows:, :].astype(f32)
                logs[0:1, pl.ds(start, share)] = tail[0:1] + tail[1:2] + tail[2:3]
                if c == 0:
                    center = center + (tail[3:4] + tail[4:5] + tail[5:6])
        center3 = split(center[:, :LANES], 3)
        line = lax.broadcasted_iota(jnp.int32, (2 * ROWS, LANES), 0)
        first = lax.broadcasted_iota(jnp.int32, (2 * ROWS, LANES), 1) < kinds
        stack = jnp.zeros((2 * ROWS, LANES), f32)
        for i, part in enumerate(center3):
            stack = jnp.where((line == i) & first, part.astype(f32), stack)
        moved = dot(stack.astype(bf16), weighted[:, pixels:], NT)
        logs[...] = logs[...] + scale * jnp.sum(moved, axis=0, keepdims=True)

    zero = jnp.zeros((), bf16)
    for g in range(0, groups, 2):
        dense = []
        for q in range(2):
            group = step * groups + g + q
            dense.append(
                jnp.where(names[0:1, :] == group, weights[:pairs, :], zero)
                + jnp.where(names[1:2, :] == group, weights[pairs:, :], zero)
            )
        value = dot(jnp.concatenate(dense, axis=0), weighted[...], NN)
        for i in range(turns):
            for t in range(tiles):
                pair = [
                    value[q * pairs + i * ROWS:q * pairs + (i + 1) * ROWS, t * LANES:(t + 1) * LANES]
                    for q in range(2)
                ]
                at = (t * groups + g) * ROWS
                lhs[at:at + 2 * ROWS, i * LANES:(i + 1) * LANES] = jnp.concatenate(pair, axis=0).astype(bf16)
            for q in range(2):
                by_kind[(g + q) * ROWS:(g + q + 1) * ROWS, i * kinds:(i + 1) * kinds] = value[
                    q * pairs + i * ROWS:q * pairs + (i + 1) * ROWS, pixels:pixels + kinds
                ]
    total = dot(lhs[...], matrix[...], NN)
    heavy = dot(jnp.concatenate(split(by_kind[...], 2), axis=0), response[...], NN)
    heavy = heavy[:groups * ROWS] + heavy[groups * ROWS:]
    upper = lax.broadcasted_iota(jnp.int32, (ROWS, LANES), 0) < cpg

    def fold(parts):
        out = parts[0]
        for j in range(1, pack):
            out = out + pltpu.roll(parts[j], ROWS - j * cpg, 0)
        return out

    for g in range(groups):
        for t in range(tiles):
            at = slice((t * groups + g) * ROWS, (t * groups + g + 1) * ROWS)
            top = fold([total[at, j * LANES:(j + 1) * LANES] for j in range(pack)])
            at = slice(g * ROWS, (g + 1) * ROWS)
            low = fold(
                [heavy[at, j * pixels + t * LANES:j * pixels + (t + 1) * LANES] for j in range(pack)]
            )
            sums[at, t * LANES:(t + 1) * LANES] = jnp.where(upper, top, pltpu.roll(low, cpg, 0))


def collect(blocks, chunks, names, weighted, matrix, response, me, turn_count, kinds, group_pairs, groups, groups_all, scale):
    count, width = weighted.shape
    pixels = width - LANES
    peers = len(blocks) // chunks
    steps = groups_all // groups
    turns = matrix.shape[0] // LANES
    return pl.pallas_call(
        functools.partial(collect_kernel, groups, turn_count, kinds, scale, peers, chunks),
        grid=(steps,),
        in_specs=[SMEM]
        + [same_spec(steps, a.shape) for a in (names, weighted, matrix, response)]
        + [same_spec(steps, b.shape) for b in blocks],
        out_specs=[block_spec(steps, (groups * ROWS, pixels), 0), same_spec(steps, (1, count))],
        out_shape=[
            jax.ShapeDtypeStruct((groups_all * ROWS, pixels), f32),
            jax.ShapeDtypeStruct((1, count), f32),
        ],
        scratch_shapes=[
            pltpu.VMEM((2 * group_pairs, count), bf16),
            pltpu.VMEM((pixels // LANES * groups * ROWS, turns * LANES), bf16),
            pltpu.VMEM((groups * ROWS, turns * kinds), f32),
        ],
        name="collect",
        **limits(32, 2 * groups_all * group_pairs * width * count, 4 * count * pixels),
    )(me, names, weighted, matrix, response, *blocks)


def swap(x, axis, k):
    return lax.ppermute(x, axis, [(i, i ^ k) for i in range(lax.axis_size(axis))])


def paired(size):
    return size & (size - 1) == 0 and 2 <= size <= 8


def place(group, size):
    if not paired(size):
        return group
    apart = group ^ lax.axis_index("dom").astype(group.dtype)
    return (apart & 1) * (size // 2) + (apart >> 1)


def gather_dom(x, size):
    if not paired(size):
        return lax.all_gather(x, "dom", axis=0, tiled=True)
    half = jnp.concatenate([x] + [swap(x, "dom", 2 * k) for k in range(1, size // 2)], axis=0)
    return jnp.concatenate([half, swap(half, "dom", 1)], axis=0)


def scatter_dom(x, size):
    if not paired(size):
        return lax.psum_scatter(x, "dom", scatter_dimension=0, tiled=True)
    half = x.shape[0] // 2
    rows = x.shape[0] // size
    x = x[:half] + swap(x[half:], "dom", 1)
    total = x[:rows]
    for k in range(1, size // 2):
        total = total + swap(x[k * rows:(k + 1) * rows], "dom", 2 * k)
    return total


def local(particles, candidates, defocus, ctf_table, references, rotations):
    count, pixels = particles.shape
    peers = lax.axis_size("cls")
    owners = lax.axis_size("dom")
    turn_count = rotations.shape[0]
    cpg = references.shape[0]
    pack = ROWS // cpg
    group_pairs = cpg * turn_count
    groups = math.gcd(owners, 8)
    kinds = ctf_table.shape[0]
    scale = 4.0 / math.sqrt(pixels * peers)
    me = lax.axis_index("cls").astype(jnp.int32).reshape(1)
    kind = defocus.reshape(1, count)
    names = place(candidates.T, owners)
    refs = gather_dom(jnp.concatenate([references] * pack, axis=0), owners)
    matrix, response = prepare(rotations, ctf_table, pack)
    weighted = weigh(particles, kind, ctf_table)
    rotated, mean = rotate(refs, matrix, ctf_table, turn_count, groups)
    chunks = 2
    size = count // chunks
    blocks = []
    for c in range(chunks):
        at = slice(c * size, (c + 1) * size)
        cut = score(weighted[at], names[:, at], rotated, me, peers, group_pairs, groups, scale)
        total = cut[0]
        for k in range(1, peers):
            total = total + swap(cut[k].astype(jnp.float16), "cls", k).astype(f32)
        own = soften(total, mean)
        blocks.extend([own] + [swap(own, "cls", k) for k in range(1, peers)])
    sums, logs = collect(
        blocks, chunks, names, weighted, matrix, response, me, turn_count, kinds, group_pairs, groups, owners, scale
    )
    total = scatter_dom(sums, owners)
    return total[:cpg].astype(bf16), total[cpg:], logs.reshape(count)


def solution(mesh):
    in_specs = (P("dom", "cls"), P("dom", None), P("dom"), P(None, "cls"), P("dom", "cls"), P())
    out_specs = (P("dom", "cls"), P("dom", "cls"), P("dom"))
    return jax.shard_map(local, mesh=mesh, in_specs=in_specs, out_specs=out_specs, check_vma=False)
```

```python
import functools
import math

import jax
import jax.numpy as jnp
from jax import lax
from jax.experimental import pallas as pl
from jax.experimental.pallas import tpu as pltpu
from jax.sharding import PartitionSpec as P

f32, bf16 = jnp.float32, jnp.bfloat16
VMEM = pl.BlockSpec(memory_space=pltpu.VMEM)
SMEM = pl.BlockSpec(memory_space=pltpu.SMEM)
HBM = pl.BlockSpec(memory_space=pltpu.HBM)
LANES, ROWS = 128, 8
NN = (((1,), (0,)), ((), ()))
NT = (((1,), (1,)), ((), ()))


def dot(a, b, dims):
    return lax.dot_general(a, b, dims, preferred_element_type=f32)


def split(x, parts):
    out = []
    for _ in range(parts):
        out.append(x.astype(bf16))
        x = x - out[-1].astype(f32)
    return out


def limits(mib, flops, moved, transcendentals=0):
    return dict(
        compiler_params=pltpu.CompilerParams(vmem_limit_bytes=mib << 20),
        cost_estimate=pl.CostEstimate(flops=flops, bytes_accessed=moved, transcendentals=transcendentals),
    )


def block_spec(steps, shape, dim):
    if steps == 1:
        return VMEM
    index = lambda i: tuple(i if d == dim else 0 for d in range(len(shape)))
    return pl.BlockSpec(shape, index)


def same_spec(steps, shape):
    return VMEM if steps == 1 else pl.BlockSpec(shape, lambda i: (0,) * len(shape))


def start_kernel(pack, pixels_in, turns_in, table_in, kind_in, names_in, *rest):
    matrix, response, weighted, power_out, names = rest[:5]
    pixels, turns, table, kind, done = rest[5:]
    moves = [
        pltpu.make_async_copy(source, target, done.at[i])
        for i, (source, target) in enumerate(
            [(turns_in, turns), (table_in, table), (kind_in, kind), (names_in, names), (pixels_in, pixels)]
        )
    ]
    for move in moves:
        move.start()
    turn_count, angles, _ = turns.shape
    kinds, width = table.shape
    per = LANES // angles
    tiles = width // LANES
    row = lax.broadcasted_iota(jnp.int32, (LANES, LANES), 0) // angles
    col = lax.broadcasted_iota(jnp.int32, (LANES, LANES), 1) // angles
    zero = jnp.zeros((), bf16)
    moves[0].wait()
    moves[1].wait()
    power = split(table[...] * table[...], 2)
    power_out[...] = jnp.concatenate(power, axis=0)
    lhs = jnp.concatenate(
        [
            jnp.concatenate([part[:, t * LANES:(t + 1) * LANES] for part in power], axis=1)
            for t in range(tiles)
        ],
        axis=0,
    )
    for i in range(turn_count // pack):
        wide = []
        for j in range(pack):
            turn = turns[i * pack + j]
            turn = jnp.concatenate([jnp.concatenate([turn] * per, axis=1)] * per, axis=0)
            wide.append(jnp.where(row == col, turn, zero))
        wide = jnp.concatenate(wide, axis=1)
        matrix[i * LANES:(i + 1) * LANES, :] = wide
        value = dot(lhs, jnp.concatenate([wide, wide], axis=0), NN).astype(bf16)
        for j in range(pack):
            for t in range(tiles):
                response[i * kinds:(i + 1) * kinds, j * width + t * LANES:j * width + (t + 1) * LANES] = value[
                    t * kinds:(t + 1) * kinds, j * LANES:(j + 1) * LANES
                ]
    for move in moves[2:]:
        move.wait()
    table3 = jnp.concatenate(split(table[...], 3), axis=0)
    count = pixels.shape[0]
    rows = math.gcd(count, 256)
    ids = lax.broadcasted_iota(jnp.int32, (LANES, rows), 0)
    for i in range(count // rows):
        at = slice(i * rows, (i + 1) * rows)
        hit = jnp.where((ids % kinds == kind[:, at]) & (ids < 3 * kinds), 1.0, 0.0).T.astype(bf16)
        factor = dot(hit[:, :3 * kinds], table3, NN)
        weighted[at, :width] = (pixels[at, :].astype(f32) * factor).astype(bf16)
        weighted[at, width:] = hit


def start(particles, turns, table, kind, names, pack):
    count, pixels = particles.shape
    turn_count, angles, _ = turns.shape
    kinds = table.shape[0]
    steps = turn_count // pack
    return pl.pallas_call(
        functools.partial(start_kernel, pack),
        in_specs=[HBM] * 5,
        out_specs=[VMEM] * 5,
        out_shape=[
            jax.ShapeDtypeStruct((steps * LANES, pack * LANES), bf16),
            jax.ShapeDtypeStruct((steps * kinds, pack * pixels), bf16),
            jax.ShapeDtypeStruct((count, pixels + LANES), bf16),
            jax.ShapeDtypeStruct((2 * kinds, pixels), bf16),
            jax.ShapeDtypeStruct(names.shape, jnp.int32),
        ],
        scratch_shapes=[
            pltpu.VMEM(particles.shape, bf16),
            pltpu.VMEM(turns.shape, bf16),
            pltpu.VMEM(table.shape, f32),
            pltpu.VMEM(kind.shape, jnp.int32),
            pltpu.SemaphoreType.DMA((5,)),
        ],
        name="start",
        **limits(12, 8 * steps * kinds * pack * pixels * LANES, 4 * count * pixels),
    )(particles, turns, table, kind, names)


def pack_kernel(own, other, out):
    rows = own.shape[0]
    out[:rows, :] = own[...]
    out[rows:, :] = other[...]


def pack_pair(own, other):
    return pl.pallas_call(
        pack_kernel,
        in_specs=[VMEM, VMEM],
        out_specs=VMEM,
        out_shape=jax.ShapeDtypeStruct((2 * own.shape[0], own.shape[1]), own.dtype),
        name="pack_pair",
        **limits(4, 0, 4 * own.size),
    )(own, other)


def rotate_kernel(groups, turn_count, power2, matrix, *rest):
    refs = rest[:-4]
    rotated, mean, center, energy = rest[-4:]
    kinds, pixels = power2.shape[0] // 2, power2.shape[1]
    pack = matrix.shape[1] // LANES
    cpg = ROWS // pack
    tiles = pixels // LANES
    group_pairs = cpg * turn_count
    if len(refs) > 1:
        source = jnp.concatenate([block[...].astype(f32) for block in refs], axis=0)
    else:
        source = refs[0][...].astype(f32)
    line = lax.broadcasted_iota(jnp.int32, (ROWS, pixels), 0) // cpg
    copies = []
    for i in range(groups // pack):
        tile = source[i * ROWS:(i + 1) * ROWS, :]
        for k in range(pack):
            out = tile
            for j in range(pack):
                if j != k:
                    out = jnp.where(line == j, pltpu.roll(tile, (j - k) % pack * cpg, 0), out)
            copies.append(out)
    source = jnp.concatenate(copies, axis=0)
    inside = lax.broadcasted_iota(jnp.int32, (groups * ROWS, LANES), 0) % ROWS // cpg
    lhs = jnp.concatenate(
        [
            jnp.concatenate(
                [jnp.where(inside == j, source[:, t * LANES:(t + 1) * LANES], 0.0) for j in range(pack)], axis=1
            )
            for t in range(tiles)
        ],
        axis=0,
    ).astype(bf16)
    for s in range(turn_count // (2 * pack)):
        value = dot(lhs, matrix[s * 2 * LANES:(s + 1) * 2 * LANES, :], NT)
        for t in range(tiles):
            for g in range(groups):
                at = (t * groups + g) * ROWS
                pair = [value[at:at + ROWS, h * LANES:(h + 1) * LANES] for h in range(2)]
                to = g * group_pairs + s * 2 * ROWS
                rotated[to:to + 2 * ROWS, t * LANES:(t + 1) * LANES] = jnp.concatenate(pair, axis=0).astype(bf16)
    power = power2[...]
    pairs = groups * group_pairs
    rows = math.gcd(pairs, 256)
    summed = jnp.zeros((kinds, 1), f32)
    for i in range(pairs // rows):
        at = slice(i * rows, (i + 1) * rows)
        value = rotated[at, :pixels].astype(f32)
        hi, lo = split(value * value, 2)
        total = dot(power, hi, NT) + dot(power, lo, NT)
        total = -0.5 * (total[:kinds] + total[kinds:])
        energy[:, at] = total
        summed = summed + jnp.sum(total, axis=1, keepdims=True)

    @pl.when(pl.program_id(0) == 0)
    def _():
        center[...] = summed * (1.0 / pairs)

    spread = lax.broadcasted_iota(jnp.int32, (kinds, LANES), 0) == lax.broadcasted_iota(jnp.int32, (kinds, LANES), 1)
    mean[...] = jnp.sum(jnp.where(spread, center[...], 0.0), axis=0, keepdims=True)
    blank = jnp.zeros((LANES - 3 * kinds, LANES), f32)
    for i in range(pairs // LANES):
        at = slice(i * LANES, (i + 1) * LANES)
        parts = [part.astype(f32) for part in split(energy[:, at] - center[...], 3)]
        rotated[at, pixels:] = jnp.concatenate(parts + [blank], axis=0).T.astype(bf16)


def rotate(refs, matrix, power2, turn_count, groups):
    kinds, pixels = power2.shape[0] // 2, power2.shape[1]
    cpg = ROWS * LANES // matrix.shape[1]
    groups_all = sum(block.shape[0] for block in refs) // cpg
    steps = groups_all // groups
    pairs = groups * cpg * turn_count
    return pl.pallas_call(
        functools.partial(rotate_kernel, groups, turn_count),
        grid=(steps,),
        in_specs=[same_spec(steps, power2.shape), same_spec(steps, matrix.shape)]
        + [block_spec(steps, (block.shape[0] // steps, pixels), 0) for block in refs],
        out_specs=[block_spec(steps, (pairs, pixels + LANES), 0), same_spec(steps, (1, LANES))],
        out_shape=[
            jax.ShapeDtypeStruct((steps * pairs, pixels + LANES), bf16),
            jax.ShapeDtypeStruct((1, LANES), f32),
        ],
        scratch_shapes=[pltpu.VMEM((kinds, 1), f32), pltpu.VMEM((kinds, pairs), f32)],
        name="rotate",
        **limits(12 if steps == 1 else 32, 8 * steps * pairs * pixels * 64, 2 * steps * pairs * pixels),
    )(power2, matrix, *refs)


def score_kernel(groups, scale, begin, me, here, weighted, names, rotated, *rest):
    outs, acc = rest[:-1], rest[-1]
    step = pl.program_id(0)
    count = acc.shape[1]
    pairs = rotated.shape[0] // groups
    span = math.gcd(count, 256)
    for n in range(count // span):
        cols = slice(n * span, (n + 1) * span)
        at = slice(begin + n * span, begin + (n + 1) * span)
        pix = weighted[at, :]
        for g in range(groups):
            value = scale * dot(rotated[g * pairs:(g + 1) * pairs, :], pix, NT)
            group = (step * groups + g) ^ here[0]
            for k in range(2):
                rows = slice(k * pairs, (k + 1) * pairs)
                hit = names[k:k + 1, at] == group
                if g == 0:
                    hit = hit | (step == 0)
                acc[rows, cols] = jnp.where(hit, value, acc[rows, cols])

    @pl.when(step == pl.num_programs(0) - 1)
    def _():
        share = outs[0].shape[1]
        for k, out in enumerate(outs):
            start = pl.multiple_of((me[0] ^ k) * share, share)
            out[...] = acc[:, pl.ds(start, share)]


def score(begin, count, weighted, names, rotated, me, here, peers, group_pairs, groups, scale):
    width = weighted.shape[1]
    steps = rotated.shape[0] // (group_pairs * groups)
    share = count // peers
    rows = 2 * group_pairs
    return pl.pallas_call(
        functools.partial(score_kernel, groups, scale, begin),
        grid=(steps,),
        in_specs=[
            SMEM,
            SMEM,
            same_spec(steps, weighted.shape),
            same_spec(steps, names.shape),
            block_spec(steps, (groups * group_pairs, width), 0),
        ],
        out_specs=[same_spec(steps, (rows, share))] * peers,
        out_shape=[jax.ShapeDtypeStruct((rows, share), f32)] * peers,
        scratch_shapes=[pltpu.VMEM((rows, count), f32)],
        name="score",
        **limits(12 if steps == 1 else 32, 2 * rotated.shape[0] * width * count, 2 * rotated.shape[0] * width),
    )(me, here, weighted, names, rotated)


def soften_kernel(scores, mean, out):
    value = scores[...]
    rows, share = value.shape
    top = jnp.max(value, axis=0, keepdims=True)
    grown = jnp.exp(value - top)
    total = jnp.sum(grown, axis=0, keepdims=True)
    out[:rows, :] = (grown * (1.0 / total)).astype(bf16)
    tail = jnp.zeros((2 * ROWS, share), f32)
    at = lax.broadcasted_iota(jnp.int32, tail.shape, 0)
    centers = mean[...]
    if share > LANES:
        centers = jnp.concatenate([centers, jnp.zeros((1, share - LANES), f32)], axis=1)
    for i, row in enumerate(split(top + jnp.log(total), 3) + split(centers, 3)):
        tail = jnp.where(at == i, row.astype(f32), tail)
    out[rows:, :] = tail.astype(bf16)


def soften(scores, mean):
    rows, share = scores.shape
    return pl.pallas_call(
        soften_kernel,
        in_specs=[VMEM, VMEM],
        out_specs=VMEM,
        out_shape=jax.ShapeDtypeStruct((rows + 2 * ROWS, share), bf16),
        name="soften",
        **limits(8, 4 * rows * share, 6 * rows * share, rows * share),
    )(scores, mean)


def collect_kernel(groups, parts, turn_count, kinds, scale, begin, peers, more, me, here, names, weighted, *rest):
    matrix, response = rest[:2]
    blocks = rest[2:2 + peers]
    before = rest[2 + peers:2 + peers + (parts + 1) * more]
    sums = rest[2 + peers + (parts + 1) * more:][:parts]
    logs, weights, lhs, by_kind = rest[-4:]
    step = pl.program_id(0)
    pixels = weighted.shape[1] - LANES
    share = blocks[0].shape[1]
    count = share * peers
    rows = weights.shape[0]
    pairs = rows // 2
    pack = matrix.shape[1] // LANES
    cpg = ROWS // pack
    tiles = pixels // LANES
    turns = turn_count // pack
    own = slice(begin, begin + count)

    @pl.when(step == 0)
    def _():
        center = jnp.zeros((1, share), f32)
        for k, block in enumerate(blocks):
            start = pl.multiple_of((me[0] ^ k) * share, share)
            weights[:, pl.ds(start, share)] = block[:rows, :]
            tail = block[rows:, :].astype(f32)
            logs[0:1, pl.ds(begin + start, share)] = tail[0:1] + tail[1:2] + tail[2:3]
            center = center + (tail[3:4] + tail[4:5] + tail[5:6])
        line = lax.broadcasted_iota(jnp.int32, (2 * ROWS, LANES), 0)
        first = lax.broadcasted_iota(jnp.int32, (2 * ROWS, LANES), 1) < kinds
        stack = jnp.zeros((2 * ROWS, LANES), f32)
        for i, part in enumerate(split(center[:, :LANES], 3)):
            stack = jnp.where((line == i) & first, part.astype(f32), stack)
        moved = dot(stack.astype(bf16), weighted[own, pixels:], NT)
        logs[:, own] = logs[:, own] + scale * jnp.sum(moved, axis=0, keepdims=True)
        if more:
            logs[:, :begin] = before[-1][:, :begin]

    zero = jnp.zeros((), bf16)
    for g in range(0, groups, 2):
        dense = []
        for q in range(2):
            group = (step * groups + g + q) ^ here[0]
            dense.append(
                jnp.where(names[0:1, own] == group, weights[:pairs, :], zero)
                + jnp.where(names[1:2, own] == group, weights[pairs:, :], zero)
            )
        value = dot(jnp.concatenate(dense, axis=0), weighted[own, :], NN)
        for i in range(turns):
            for t in range(tiles):
                pair = [
                    value[q * pairs + i * ROWS:q * pairs + (i + 1) * ROWS, t * LANES:(t + 1) * LANES]
                    for q in range(2)
                ]
                at = (t * groups + g) * ROWS
                lhs[at:at + 2 * ROWS, i * LANES:(i + 1) * LANES] = jnp.concatenate(pair, axis=0).astype(bf16)
            for q in range(2):
                by_kind[(g + q) * ROWS:(g + q + 1) * ROWS, i * kinds:(i + 1) * kinds] = value[
                    q * pairs + i * ROWS:q * pairs + (i + 1) * ROWS, pixels:pixels + kinds
                ]
    total = dot(lhs[...], matrix[...], NN)
    heavy = dot(jnp.concatenate(split(by_kind[...], 2), axis=0), response[...], NN)
    heavy = heavy[:groups * ROWS] + heavy[groups * ROWS:]
    upper = lax.broadcasted_iota(jnp.int32, (ROWS, LANES), 0) < cpg

    def fold(terms):
        out = terms[0]
        for j in range(1, pack):
            out = out + pltpu.roll(terms[j], ROWS - j * cpg, 0)
        return out

    for g in range(groups):
        to = slice(g // parts * ROWS, (g // parts + 1) * ROWS)
        for t in range(tiles):
            lanes = slice(t * LANES, (t + 1) * LANES)
            at = slice((t * groups + g) * ROWS, (t * groups + g + 1) * ROWS)
            top = fold([total[at, j * LANES:(j + 1) * LANES] for j in range(pack)])
            at = slice(g * ROWS, (g + 1) * ROWS)
            low = fold(
                [heavy[at, j * pixels + t * LANES:j * pixels + (t + 1) * LANES] for j in range(pack)]
            )
            value = jnp.where(upper, top, pltpu.roll(low, cpg, 0))
            if more:
                value = value + before[g % parts][to, lanes]
            sums[g % parts][to, lanes] = value


def collect(
    begin, blocks, before, names, weighted, matrix, response, me, here, parts, turn_count, kinds, group_pairs, groups,
    groups_all, scale
):
    count, width = weighted.shape
    pixels = width - LANES
    peers = len(blocks)
    steps = groups_all // groups
    turns = matrix.shape[0] // LANES
    rows = groups * ROWS // parts
    sums_spec = [block_spec(steps, (rows, pixels), 0)] * parts
    return pl.pallas_call(
        functools.partial(
            collect_kernel, groups, parts, turn_count, kinds, scale, begin, peers, 1 if before else 0
        ),
        grid=(steps,),
        in_specs=[SMEM, SMEM]
        + [same_spec(steps, a.shape) for a in (names, weighted, matrix, response)]
        + [same_spec(steps, b.shape) for b in blocks]
        + (sums_spec + [same_spec(steps, (1, count))] if before else []),
        out_specs=sums_spec + [same_spec(steps, (1, count))],
        out_shape=[jax.ShapeDtypeStruct((steps * rows, pixels), f32)] * parts
        + [jax.ShapeDtypeStruct((1, count), f32)],
        scratch_shapes=[
            pltpu.VMEM((2 * group_pairs, peers * blocks[0].shape[1]), bf16),
            pltpu.VMEM((pixels // LANES * groups * ROWS, turns * LANES), bf16),
            pltpu.VMEM((groups * ROWS, turns * kinds), f32),
        ],
        name="collect",
        **limits(
            20 if steps == 1 else 40, 2 * groups_all * group_pairs * width * peers * blocks[0].shape[1],
            4 * count * pixels
        ),
    )(me, here, names, weighted, matrix, response, *blocks, *before)


def add_kernel(left, right, *outs):
    rows = outs[0].shape[0]
    for i, out in enumerate(outs):
        at = slice(i * rows, (i + 1) * rows)
        out[...] = left[at, :] + right[at, :]


def add_cut(left, right, pieces):
    shape = (left.shape[0] // pieces, left.shape[1])
    return pl.pallas_call(
        add_kernel,
        in_specs=[VMEM, VMEM],
        out_specs=[VMEM] * pieces,
        out_shape=[jax.ShapeDtypeStruct(shape, f32)] * pieces,
        name="add_cut",
        **limits(4, left.size, 12 * left.size),
    )(left, right)


def finish_kernel(*refs):
    sums, weights = refs[-2:]
    total = refs[0][...]
    for ref in refs[1:-2]:
        total = total + ref[...]
    sums[...] = total[:sums.shape[0], :].astype(bf16)
    weights[...] = total[sums.shape[0]:, :]


def finish(pieces, cpg):
    shape = (cpg, pieces[0].shape[1])
    return pl.pallas_call(
        finish_kernel,
        in_specs=[VMEM] * len(pieces),
        out_specs=[VMEM] * 2,
        out_shape=[jax.ShapeDtypeStruct(shape, bf16), jax.ShapeDtypeStruct(shape, f32)],
        name="finish",
        **limits(4, pieces[0].size, 12 * pieces[0].size),
    )(*pieces)


def swap(x, axis, k):
    return lax.ppermute(x, axis, [(i, i ^ k) for i in range(lax.axis_size(axis))])


def local(particles, candidates, defocus, ctf_table, references, rotations):
    count, pixels = particles.shape
    peers = lax.axis_size("cls")
    owners = lax.axis_size("dom")
    paired = owners & (owners - 1) == 0 and 4 <= owners <= 8
    turn_count = rotations.shape[0]
    cpg = references.shape[0]
    pack = ROWS // cpg
    group_pairs = cpg * turn_count
    groups = math.gcd(owners, 8)
    kinds = ctf_table.shape[0]
    scale = 4.0 / math.sqrt(pixels * peers)
    me = lax.axis_index("cls").astype(jnp.int32).reshape(1)
    here = lax.axis_index("dom").astype(jnp.int32).reshape(1)
    if paired:
        pair = pack_pair(references, swap(references, "dom", 1))
        refs = [pair] + [swap(pair, "dom", 2 * k) for k in range(1, owners // 2)]
    else:
        here = jnp.zeros_like(here)
        refs = [lax.all_gather(references, "dom", axis=0, tiled=True)]
    matrix, response, weighted, power2, names = start(
        particles, rotations, ctf_table, defocus.reshape(1, count), candidates.T, pack
    )
    rotated, mean = rotate(refs, matrix, power2, turn_count, groups)
    chunks = 2
    size = count // chunks
    blocks = []
    for c in range(chunks):
        cut = score(c * size, size, weighted, names, rotated, me, here, peers, group_pairs, groups, scale)
        total = cut[0]
        for k in range(1, peers):
            total = total + swap(cut[k].astype(jnp.float16), "cls", k).astype(f32)
        own = soften(total, mean)
        blocks.append([own] + [swap(own, "cls", k) for k in range(1, peers)])
    parts = 2 if paired else 1
    out = []
    for c in range(chunks):
        out = collect(
            c * size, blocks[c], out, names, weighted, matrix, response, me, here, parts, turn_count, kinds,
            group_pairs, groups, owners, scale
        )
    if paired:
        pieces = add_cut(out[0], swap(out[1], "dom", 1), owners // 2)
        pieces = [pieces[0]] + [swap(pieces[k], "dom", 2 * k) for k in range(1, owners // 2)]
    else:
        pieces = [lax.psum_scatter(out[0], "dom", scatter_dimension=0, tiled=True)]
    class_sums, class_weights = finish(pieces, cpg)
    return class_sums, class_weights, out[-1].reshape(count)


def solution(mesh):
    in_specs = (P("dom", "cls"), P("dom", None), P("dom"), P(None, "cls"), P("dom", "cls"), P())
    out_specs = (P("dom", "cls"), P("dom", "cls"), P("dom"))
    return jax.shard_map(local, mesh=mesh, in_specs=in_specs, out_specs=out_specs, check_vma=False)
```

```python
import functools
import math

import jax
import jax.numpy as jnp
from jax import lax
from jax.experimental import pallas as pl
from jax.experimental.pallas import tpu as pltpu
from jax.sharding import PartitionSpec as P

f32, bf16 = jnp.float32, jnp.bfloat16
VMEM = pl.BlockSpec(memory_space=pltpu.VMEM)
SMEM = pl.BlockSpec(memory_space=pltpu.SMEM)
HBM = pl.BlockSpec(memory_space=pltpu.HBM)
LANES, ROWS = 128, 8
START_MIB = 16
NN = (((1,), (0,)), ((), ()))
NT = (((1,), (1,)), ((), ()))


def dot(a, b, dims):
    return lax.dot_general(a, b, dims, preferred_element_type=f32)


def split(x, parts):
    out = []
    for _ in range(parts):
        out.append(x.astype(bf16))
        x = x - out[-1].astype(f32)
    return out


def limits(mib, flops, moved, transcendentals=0):
    return dict(
        compiler_params=pltpu.CompilerParams(vmem_limit_bytes=mib << 20),
        cost_estimate=pl.CostEstimate(flops=flops, bytes_accessed=moved, transcendentals=transcendentals),
    )


def group_at(place, here):
    return place ^ here[0]


def block_spec(steps, shape, dim):
    if steps == 1:
        return VMEM
    index = lambda i: tuple(i if d == dim else 0 for d in range(len(shape)))
    return pl.BlockSpec(shape, index)


def same_spec(steps, shape):
    return VMEM if steps == 1 else pl.BlockSpec(shape, lambda i: (0,) * len(shape))


def start_kernel(pack, pixels_in, turns_in, table_in, kind_in, names_in, *rest):
    matrix, response_out, weighted, power_out, names = rest[:5]
    pixels, turns, table, kind, response, done, sent = rest[5:]
    moves = [
        pltpu.make_async_copy(source, target, done.at[i])
        for i, (source, target) in enumerate(
            [(turns_in, turns), (table_in, table), (kind_in, kind), (names_in, names), (pixels_in, pixels)]
        )
    ]
    for move in moves:
        move.start()
    turn_count, angles, _ = turns.shape
    kinds, width = table.shape
    per = LANES // angles
    tiles = width // LANES
    row = lax.broadcasted_iota(jnp.int32, (LANES, LANES), 0) // angles
    col = lax.broadcasted_iota(jnp.int32, (LANES, LANES), 1) // angles
    zero = jnp.zeros((), bf16)
    moves[0].wait()
    moves[1].wait()
    power = split(table[...] * table[...], 2)
    power_out[...] = jnp.concatenate(power, axis=0)
    lhs = jnp.concatenate(
        [
            jnp.concatenate([part[:, t * LANES:(t + 1) * LANES] for part in power], axis=1)
            for t in range(tiles)
        ],
        axis=0,
    )
    steps = turn_count // pack
    bands = math.gcd(steps, 4)
    sends = []
    for i in range(steps):
        wide = []
        for j in range(pack):
            turn = turns[i * pack + j]
            turn = jnp.concatenate([jnp.concatenate([turn] * per, axis=1)] * per, axis=0)
            wide.append(jnp.where(row == col, turn, zero))
        wide = jnp.concatenate(wide, axis=1)
        matrix[i * LANES:(i + 1) * LANES, :] = wide
        value = dot(lhs, jnp.concatenate([wide, wide], axis=0), NN).astype(bf16)
        for j in range(pack):
            for t in range(tiles):
                response[i * kinds:(i + 1) * kinds, j * width + t * LANES:j * width + (t + 1) * LANES] = value[
                    t * kinds:(t + 1) * kinds, j * LANES:(j + 1) * LANES
                ]
        if (i + 1) % (steps // bands) == 0:
            band = len(sends)
            at = pl.ds(band * (steps // bands) * kinds, steps // bands * kinds)
            send = pltpu.make_async_copy(response.at[at, :], response_out.at[at, :], sent.at[band])
            send.start()
            sends.append(send)
    for move in moves[2:]:
        move.wait()
    table3 = jnp.concatenate(split(table[...], 3), axis=0)
    count = pixels.shape[0]
    rows = math.gcd(count, 256)
    ids = lax.broadcasted_iota(jnp.int32, (LANES, rows), 0)
    for i in range(count // rows):
        at = slice(i * rows, (i + 1) * rows)
        hit = jnp.where((ids % kinds == kind[:, at]) & (ids < 3 * kinds), 1.0, 0.0).T.astype(bf16)
        factor = dot(hit[:, :3 * kinds], table3, NN)
        weighted[at, :width] = (pixels[at, :].astype(f32) * factor).astype(bf16)
        weighted[at, width:] = hit
    for send in sends:
        send.wait()


def start(particles, turns, table, kind, names, pack):
    count, pixels = particles.shape
    turn_count, angles, _ = turns.shape
    kinds = table.shape[0]
    steps = turn_count // pack
    return pl.pallas_call(
        functools.partial(start_kernel, pack),
        in_specs=[HBM] * 5,
        out_specs=[VMEM, HBM, VMEM, VMEM, VMEM],
        out_shape=[
            jax.ShapeDtypeStruct((steps * LANES, pack * LANES), bf16),
            jax.ShapeDtypeStruct((steps * kinds, pack * pixels), bf16),
            jax.ShapeDtypeStruct((count, pixels + LANES), bf16),
            jax.ShapeDtypeStruct((2 * kinds, pixels), bf16),
            jax.ShapeDtypeStruct(names.shape, jnp.int32),
        ],
        scratch_shapes=[
            pltpu.VMEM(particles.shape, bf16),
            pltpu.VMEM(turns.shape, bf16),
            pltpu.VMEM(table.shape, f32),
            pltpu.VMEM(kind.shape, jnp.int32),
            pltpu.VMEM((steps * kinds, pack * pixels), bf16),
            pltpu.SemaphoreType.DMA((5,)),
            pltpu.SemaphoreType.DMA((4,)),
        ],
        name="start",
        **limits(START_MIB, 1000000, 0),
    )(particles, turns, table, kind, names)


def stack_kernel(*refs):
    out = refs[-1]
    rows = refs[0].shape[0]
    for i, ref in enumerate(refs[:-1]):
        out[i * rows:(i + 1) * rows, :] = ref[...]


def stack(blocks):
    rows, columns = blocks[0].shape
    return pl.pallas_call(
        stack_kernel,
        in_specs=[VMEM] * len(blocks),
        out_specs=VMEM,
        out_shape=jax.ShapeDtypeStruct((len(blocks) * rows, columns), blocks[0].dtype),
        name="stack",
        **limits(4, 20_000_000_000, 1 << 25),
    )(*blocks)


def rotate_kernel(groups, turn_count, power2, matrix, *rest):
    refs = rest[:-4]
    rotated, mean, center, energy = rest[-4:]
    kinds, pixels = power2.shape[0] // 2, power2.shape[1]
    pack = matrix.shape[1] // LANES
    cpg = ROWS // pack
    tiles = pixels // LANES
    group_pairs = cpg * turn_count
    source = [block[...].astype(f32) for block in refs]
    if len(refs) > 1:
        source = [part[i * cpg:(i + 1) * cpg, :] for i in range(groups // len(refs)) for part in source]
    source = jnp.concatenate(source, axis=0)
    line = lax.broadcasted_iota(jnp.int32, (ROWS, pixels), 0) // cpg
    copies = []
    for i in range(groups // pack):
        tile = source[i * ROWS:(i + 1) * ROWS, :]
        for k in range(pack):
            out = tile
            for j in range(pack):
                if j != k:
                    out = jnp.where(line == j, pltpu.roll(tile, (j - k) % pack * cpg, 0), out)
            copies.append(out)
    source = jnp.concatenate(copies, axis=0)
    inside = lax.broadcasted_iota(jnp.int32, (groups * ROWS, LANES), 0) % ROWS // cpg
    lhs = jnp.concatenate(
        [
            jnp.concatenate(
                [jnp.where(inside == j, source[:, t * LANES:(t + 1) * LANES], 0.0) for j in range(pack)], axis=1
            )
            for t in range(tiles)
        ],
        axis=0,
    ).astype(bf16)
    for s in range(turn_count // (2 * pack)):
        value = dot(lhs, matrix[s * 2 * LANES:(s + 1) * 2 * LANES, :], NT)
        for t in range(tiles):
            for g in range(groups):
                at = (t * groups + g) * ROWS
                pair = [value[at:at + ROWS, h * LANES:(h + 1) * LANES] for h in range(2)]
                to = g * group_pairs + s * 2 * ROWS
                rotated[to:to + 2 * ROWS, t * LANES:(t + 1) * LANES] = jnp.concatenate(pair, axis=0).astype(bf16)
    power = power2[...]
    pairs = groups * group_pairs
    rows = math.gcd(pairs, 256)
    summed = jnp.zeros((kinds, 1), f32)
    for i in range(pairs // rows):
        at = slice(i * rows, (i + 1) * rows)
        value = rotated[at, :pixels].astype(f32)
        hi, lo = split(value * value, 2)
        total = dot(power, hi, NT) + dot(power, lo, NT)
        total = -0.5 * (total[:kinds] + total[kinds:])
        energy[:, at] = total
        summed = summed + jnp.sum(total, axis=1, keepdims=True)

    @pl.when(pl.program_id(0) == 0)
    def _():
        center[...] = summed * (1.0 / pairs)

    spread = lax.broadcasted_iota(jnp.int32, (kinds, LANES), 0) == lax.broadcasted_iota(jnp.int32, (kinds, LANES), 1)
    mean[...] = jnp.sum(jnp.where(spread, center[...], 0.0), axis=0, keepdims=True)
    blank = jnp.zeros((LANES - 3 * kinds, LANES), f32)
    for i in range(pairs // LANES):
        at = slice(i * LANES, (i + 1) * LANES)
        parts = [part.astype(f32) for part in split(energy[:, at] - center[...], 3)]
        rotated[at, pixels:] = jnp.concatenate(parts + [blank], axis=0).T.astype(bf16)


def rotate(refs, matrix, power2, turn_count, groups):
    kinds, pixels = power2.shape[0] // 2, power2.shape[1]
    cpg = ROWS * LANES // matrix.shape[1]
    groups_all = sum(block.shape[0] for block in refs) // cpg
    steps = groups_all // groups
    pairs = groups * cpg * turn_count
    return pl.pallas_call(
        functools.partial(rotate_kernel, groups, turn_count),
        grid=(steps,),
        in_specs=[same_spec(steps, power2.shape), same_spec(steps, matrix.shape)]
        + [block_spec(steps, (block.shape[0] // steps, pixels), 0) for block in refs],
        out_specs=[block_spec(steps, (pairs, pixels + LANES), 0), same_spec(steps, (1, LANES))],
        out_shape=[
            jax.ShapeDtypeStruct((steps * pairs, pixels + LANES), bf16),
            jax.ShapeDtypeStruct((1, LANES), f32),
        ],
        scratch_shapes=[pltpu.VMEM((kinds, 1), f32), pltpu.VMEM((kinds, pairs), f32)],
        name="rotate",
        **limits(12 if steps == 1 else 32, 8 * steps * pairs * pixels * 64, 2 * steps * pairs * pixels),
    )(power2, matrix, *refs)


def score_kernel(groups, scale, begin, me, here, weighted, names, rotated, *rest):
    outs, acc = rest[:-1], rest[-1]
    step = pl.program_id(0)
    count = acc.shape[1]
    pairs = rotated.shape[0] // groups
    span = math.gcd(count, 256)
    for n in range(count // span):
        cols = slice(n * span, (n + 1) * span)
        at = slice(begin + n * span, begin + (n + 1) * span)
        pix = weighted[at, :]
        for g in range(groups):
            value = scale * dot(rotated[g * pairs:(g + 1) * pairs, :], pix, NT)
            group = group_at(step * groups + g, here)
            for k in range(2):
                rows = slice(k * pairs, (k + 1) * pairs)
                hit = names[k:k + 1, at] == group
                if g == 0:
                    hit = hit | (step == 0)
                acc[rows, cols] = jnp.where(hit, value, acc[rows, cols])

    @pl.when(step == pl.num_programs(0) - 1)
    def _():
        share = outs[0].shape[1]
        for k, out in enumerate(outs):
            start = pl.multiple_of((me[0] ^ k) * share, share)
            out[...] = acc[:, pl.ds(start, share)]


def score(begin, count, weighted, names, rotated, me, here, peers, group_pairs, groups, scale):
    width = weighted.shape[1]
    steps = rotated.shape[0] // (group_pairs * groups)
    share = count // peers
    rows = 2 * group_pairs
    return pl.pallas_call(
        functools.partial(score_kernel, groups, scale, begin),
        grid=(steps,),
        in_specs=[
            SMEM,
            SMEM,
            same_spec(steps, weighted.shape),
            same_spec(steps, names.shape),
            block_spec(steps, (groups * group_pairs, width), 0),
        ],
        out_specs=[same_spec(steps, (rows, share))] * peers,
        out_shape=[jax.ShapeDtypeStruct((rows, share), f32)] * peers,
        scratch_shapes=[pltpu.VMEM((rows, count), f32)],
        name="score",
        **limits(12 if steps == 1 else 32, 2 * rotated.shape[0] * width * count, 2 * rotated.shape[0] * width),
    )(me, here, weighted, names, rotated)


def soften_kernel(scores, mean, out):
    value = scores[...]
    rows, share = value.shape
    top = jnp.max(value, axis=0, keepdims=True)
    grown = jnp.exp(value - top)
    total = jnp.sum(grown, axis=0, keepdims=True)
    out[:rows, :] = (grown * (1.0 / total)).astype(bf16)
    tail = jnp.zeros((2 * ROWS, share), f32)
    at = lax.broadcasted_iota(jnp.int32, tail.shape, 0)
    centers = mean[...]
    if share > LANES:
        centers = jnp.concatenate([centers, jnp.zeros((1, share - LANES), f32)], axis=1)
    for i, row in enumerate(split(top + jnp.log(total), 3) + split(centers, 3)):
        tail = jnp.where(at == i, row.astype(f32), tail)
    out[rows:, :] = tail.astype(bf16)


def soften(scores, mean):
    rows, share = scores.shape
    return pl.pallas_call(
        soften_kernel,
        in_specs=[VMEM, VMEM],
        out_specs=VMEM,
        out_shape=jax.ShapeDtypeStruct((rows + 2 * ROWS, share), bf16),
        name="soften",
        **limits(8, 4 * rows * share, 6 * rows * share, rows * share),
    )(scores, mean)


def collect_kernel(groups, parts, turn_count, kinds, scale, begin, peers, first, last, me, here, names, weighted, *rest):
    rest = list(rest)
    take = lambda n: [rest.pop(0) for _ in range(n)]
    matrix, response = take(2) if last else (None, None)
    blocks = take(peers)
    before = None if first else take(3)
    sums = take(parts) if last else None
    logs, weights, lhs, by_kind = rest if last else [rest[i] for i in (2, 3, 0, 1)]
    step = pl.program_id(0)
    pixels = weighted.shape[1] - LANES
    share = blocks[0].shape[1]
    count = share * peers
    rows = weights.shape[0]
    pairs = rows // 2
    turns = lhs.shape[1] // LANES
    pack = turn_count // turns
    cpg = ROWS // pack
    tiles = pixels // LANES
    own = slice(begin, begin + count)

    @pl.when(step == 0)
    def _():
        center = jnp.zeros((1, share), f32)
        for k, block in enumerate(blocks):
            start = pl.multiple_of((me[0] ^ k) * share, share)
            weights[:, pl.ds(start, share)] = block[:rows, :]
            tail = block[rows:, :].astype(f32)
            logs[0:1, pl.ds(begin + start, share)] = tail[0:1] + tail[1:2] + tail[2:3]
            center = center + (tail[3:4] + tail[4:5] + tail[5:6])
        line = lax.broadcasted_iota(jnp.int32, (2 * ROWS, LANES), 0)
        inside = lax.broadcasted_iota(jnp.int32, (2 * ROWS, LANES), 1) < kinds
        stacked = jnp.zeros((2 * ROWS, LANES), f32)
        for i, part in enumerate(split(center[:, :LANES], 3)):
            stacked = jnp.where((line == i) & inside, part.astype(f32), stacked)
        moved = dot(stacked.astype(bf16), weighted[own, pixels:], NT)
        logs[:, own] = logs[:, own] + scale * jnp.sum(moved, axis=0, keepdims=True)
        if not first:
            logs[:, :begin] = before[2][:, :begin]

    zero = jnp.zeros((), bf16)
    for g in range(0, groups, 2):
        dense = []
        for q in range(2):
            group = group_at(step * groups + g + q, here)
            dense.append(
                jnp.where(names[0:1, own] == group, weights[:pairs, :], zero)
                + jnp.where(names[1:2, own] == group, weights[pairs:, :], zero)
            )
        value = dot(jnp.concatenate(dense, axis=0), weighted[own, :], NN)
        for i in range(turns):
            lanes = slice(i * LANES, (i + 1) * LANES)
            for t in range(tiles):
                pair = [
                    value[q * pairs + i * ROWS:q * pairs + (i + 1) * ROWS, t * LANES:(t + 1) * LANES]
                    for q in range(2)
                ]
                pair = jnp.concatenate(pair, axis=0)
                at = slice((t * groups + g) * ROWS, (t * groups + g + 2) * ROWS)
                if not first:
                    pair = pair + before[0][at, lanes]
                lhs[at, lanes] = pair.astype(lhs.dtype)
            for q in range(2):
                by_kind[(g + q) * ROWS:(g + q + 1) * ROWS, i * kinds:(i + 1) * kinds] = value[
                    q * pairs + i * ROWS:q * pairs + (i + 1) * ROWS, pixels:pixels + kinds
                ]
    if not last:
        if not first:
            by_kind[...] = by_kind[...] + before[1][...]
        return
    total = dot(lhs[...], matrix[...], NN)
    light = by_kind[...] if first else by_kind[...] + before[1][...]
    heavy = dot(jnp.concatenate(split(light, 2), axis=0), response[...], NN)
    heavy = heavy[:groups * ROWS] + heavy[groups * ROWS:]
    upper = lax.broadcasted_iota(jnp.int32, (ROWS, LANES), 0) < cpg

    def fold(terms):
        out = terms[0]
        for j in range(1, pack):
            out = out + pltpu.roll(terms[j], ROWS - j * cpg, 0)
        return out

    for g in range(groups):
        part, to = g % parts, slice(g // parts * ROWS, (g // parts + 1) * ROWS)
        for t in range(tiles):
            lanes = slice(t * LANES, (t + 1) * LANES)
            at = slice((t * groups + g) * ROWS, (t * groups + g + 1) * ROWS)
            top = fold([total[at, j * LANES:(j + 1) * LANES] for j in range(pack)])
            at = slice(g * ROWS, (g + 1) * ROWS)
            low = fold(
                [heavy[at, j * pixels + t * LANES:j * pixels + (t + 1) * LANES] for j in range(pack)]
            )
            sums[part][to, lanes] = jnp.where(upper, top, pltpu.roll(low, cpg, 0))


def collect(
    begin, blocks, before, last, names, weighted, matrix, response, me, here, parts, turn_count, kinds, group_pairs,
    groups, groups_all, scale
):
    count, width = weighted.shape
    pixels = width - LANES
    peers = len(blocks)
    steps = groups_all // groups
    turns = matrix.shape[0] // LANES
    rows = groups * ROWS // parts
    first = not before
    left = (pixels // LANES * groups * ROWS, turns * LANES)
    light = (groups * ROWS, turns * kinds)
    logs_spec = same_spec(steps, (1, count))
    logs_shape = jax.ShapeDtypeStruct((1, count), f32)
    sides = [block_spec(steps, left, 0), block_spec(steps, light, 0)]
    weights_scratch = pltpu.VMEM((2 * group_pairs, peers * blocks[0].shape[1]), bf16)
    if last:
        out_specs = [block_spec(steps, (rows, pixels), 0)] * parts + [logs_spec]
        out_shape = [jax.ShapeDtypeStruct((steps * rows, pixels), f32)] * parts + [logs_shape]
        scratch = [weights_scratch, pltpu.VMEM(left, bf16), pltpu.VMEM(light, f32)]
    else:
        out_specs = sides + [logs_spec]
        out_shape = [jax.ShapeDtypeStruct((steps * shape[0], shape[1]), f32) for shape in (left, light)] + [logs_shape]
        scratch = [weights_scratch]
    both = [names, weighted] + ([matrix, response] if last else []) + blocks
    return pl.pallas_call(
        functools.partial(
            collect_kernel, groups, parts, turn_count, kinds, scale, begin, peers, first, last
        ),
        grid=(steps,),
        in_specs=[SMEM, SMEM]
        + [same_spec(steps, a.shape) for a in both]
        + ([] if first else sides + [logs_spec]),
        out_specs=out_specs,
        out_shape=out_shape,
        scratch_shapes=scratch,
        name="collect",
        **limits(
            20 if steps == 1 else 56, 2 * groups_all * group_pairs * width * peers * blocks[0].shape[1],
            4 * count * pixels
        ),
    )(me, here, *both, *before)


def add_kernel(left, right, *outs):
    rows = outs[0].shape[0]
    for i, out in enumerate(outs):
        at = slice(i * rows, (i + 1) * rows)
        out[...] = left[at, :] + right[at, :]


def add_cut(left, right, pieces):
    shape = (left.shape[0] // pieces, left.shape[1])
    return pl.pallas_call(
        add_kernel,
        in_specs=[VMEM, VMEM],
        out_specs=[VMEM] * pieces,
        out_shape=[jax.ShapeDtypeStruct(shape, f32)] * pieces,
        name="add_cut",
        **limits(4, left.size, 12 * left.size),
    )(left, right)


def finish_kernel(*refs):
    sums, weights = refs[-2:]
    total = refs[0][...]
    for ref in refs[1:-2]:
        total = total + ref[...]
    sums[...] = total[:sums.shape[0], :].astype(bf16)
    weights[...] = total[sums.shape[0]:, :]


def finish(pieces, cpg):
    shape = (cpg, pieces[0].shape[1])
    return pl.pallas_call(
        finish_kernel,
        in_specs=[VMEM] * len(pieces),
        out_specs=[VMEM] * 2,
        out_shape=[jax.ShapeDtypeStruct(shape, bf16), jax.ShapeDtypeStruct(shape, f32)],
        name="finish",
        **limits(4, pieces[0].size, 12 * pieces[0].size),
    )(*pieces)


def swap(x, axis, k):
    return lax.ppermute(x, axis, [(i, i ^ k) for i in range(lax.axis_size(axis))])


def local(particles, candidates, defocus, ctf_table, references, rotations):
    count, pixels = particles.shape
    peers = lax.axis_size("cls")
    owners = lax.axis_size("dom")
    paired = owners & (owners - 1) == 0 and 4 <= owners <= 8
    turn_count = rotations.shape[0]
    cpg = references.shape[0]
    pack = ROWS // cpg
    group_pairs = cpg * turn_count
    groups = math.gcd(owners, 8)
    kinds = ctf_table.shape[0]
    scale = 4.0 / math.sqrt(pixels * peers)
    me = lax.axis_index("cls").astype(jnp.int32).reshape(1)
    here = (lax.axis_index("dom") if paired else jnp.int32(0)).astype(jnp.int32).reshape(1)
    if paired:
        half = stack([references] + [swap(references, "dom", 2 * k) for k in range(1, owners // 2)])
        refs = [half, swap(half, "dom", 1)]
    else:
        refs = [lax.all_gather(references, "dom", axis=0, tiled=True)]
    matrix, response, weighted, power2, names = start(
        particles, rotations, ctf_table, defocus.reshape(1, count), candidates.T, pack
    )
    rotated, mean = rotate(refs, matrix, power2, turn_count, groups)
    chunks = 2
    size = count // chunks
    blocks = []
    for c in range(chunks):
        cut = score(c * size, size, weighted, names, rotated, me, here, peers, group_pairs, groups, scale)
        total = cut[0]
        for k in range(1, peers):
            total = total + swap(cut[k].astype(jnp.float16), "cls", k).astype(f32)
        own = soften(total, mean)
        blocks.append([own] + [swap(own, "cls", k) for k in range(1, peers)])
    parts = 2 if paired else 1
    out = []
    for c in range(chunks):
        out = collect(
            c * size, blocks[c], out, c == chunks - 1, names, weighted, matrix, response, me, here, parts, turn_count,
            kinds, group_pairs, groups, owners, scale
        )
    if paired:
        pieces = add_cut(out[0], swap(out[1], "dom", 1), owners // 2)
        pieces = [pieces[0]] + [swap(pieces[k], "dom", 2 * k) for k in range(1, owners // 2)]
    else:
        pieces = [lax.psum_scatter(out[0], "dom", scatter_dimension=0, tiled=True)]
    class_sums, class_weights = finish(pieces, cpg)
    return class_sums, class_weights, out[-1].reshape(count)


def solution(mesh):
    in_specs = (P("dom", "cls"), P("dom", None), P("dom"), P(None, "cls"), P("dom", "cls"), P())
    out_specs = (P("dom", "cls"), P("dom", "cls"), P("dom"))
    return jax.shard_map(local, mesh=mesh, in_specs=in_specs, out_specs=out_specs, check_vma=False)
```

```python
import functools
import math

import jax
import jax.numpy as jnp
from jax import lax
from jax.experimental import pallas as pl
from jax.experimental.pallas import tpu as pltpu
from jax.sharding import PartitionSpec as P

f32, bf16 = jnp.float32, jnp.bfloat16
VMEM = pl.BlockSpec(memory_space=pltpu.VMEM)
SMEM = pl.BlockSpec(memory_space=pltpu.SMEM)
LANES, ROWS = 128, 8
PREPARE = 1 << 20
EARLY = 20_000_000_000
NN = (((1,), (0,)), ((), ()))
NT = (((1,), (1,)), ((), ()))


def dot(a, b, dims):
    return lax.dot_general(a, b, dims, preferred_element_type=f32)


def split(x, parts):
    out = []
    for _ in range(parts):
        out.append(x.astype(bf16))
        x = x - out[-1].astype(f32)
    return out


def limits(mib, flops, moved, transcendentals=0):
    return dict(
        compiler_params=pltpu.CompilerParams(vmem_limit_bytes=mib << 20),
        cost_estimate=pl.CostEstimate(flops=flops, bytes_accessed=moved, transcendentals=transcendentals),
    )


def group_at(place, here):
    return place ^ here[0]


def block_spec(steps, shape, dim):
    if steps == 1:
        return VMEM
    index = lambda i: tuple(i if d == dim else 0 for d in range(len(shape)))
    return pl.BlockSpec(shape, index)


def same_spec(steps, shape):
    return VMEM if steps == 1 else pl.BlockSpec(shape, lambda i: (0,) * len(shape))


def turn_matrix(turns, i, pack, inside):
    _, angles, width = turns.shape
    per = LANES // angles
    wide = []
    for j in range(pack):
        turn = turns[i * pack + j]
        turn = jnp.concatenate([jnp.concatenate([turn] * (LANES // width), axis=1)] * per, axis=0)
        wide.append(jnp.where(inside, turn, jnp.zeros((), bf16)))
    return jnp.concatenate(wide, axis=1)


def same_cycle(angles):
    row = lax.broadcasted_iota(jnp.int32, (LANES, LANES), 0) // angles
    col = lax.broadcasted_iota(jnp.int32, (LANES, LANES), 1) // angles
    return row == col


def seed_kernel(out):
    out[...] = lax.broadcasted_iota(jnp.int32, out.shape, 0)


def seed():
    return pl.pallas_call(
        seed_kernel,
        out_specs=VMEM,
        out_shape=jax.ShapeDtypeStruct((LANES, 2 * LANES), jnp.int32),
        name="seed",
        **limits(4, EARLY, 0),
    )()


def start_kernel(numbers, own_in, pixels, turns, table, kind, names_in, weighted, power, names, own, turns2):
    names[...] = names_in[...]
    own[...] = own_in[...]
    for i in range(turns.shape[0]):
        turns2[i] = jnp.concatenate([turns[i]] * (LANES // turns.shape[2]), axis=1)
    kinds, width = table.shape
    power[...] = jnp.concatenate(split(table[...] * table[...], 2), axis=0)
    table3 = jnp.concatenate(split(table[...], 3), axis=0)
    count = pixels.shape[0]
    rows = math.gcd(count, 256)
    ids = numbers[:, :rows]
    for i in range(count // rows):
        at = slice(i * rows, (i + 1) * rows)
        hit = jnp.where((ids % kinds == kind[:, at]) & (ids < 3 * kinds), 1.0, 0.0).T.astype(bf16)
        factor = dot(hit[:, :3 * kinds], table3, NN)
        weighted[at, :width] = (pixels[at, :].astype(f32) * factor).astype(bf16)
        weighted[at, width:] = hit


def start(particles, references, turns, table, kind, names):
    count, pixels = particles.shape
    kinds = table.shape[0]
    return pl.pallas_call(
        start_kernel,
        in_specs=[VMEM] * 7,
        out_specs=[VMEM] * 5,
        out_shape=[
            jax.ShapeDtypeStruct((count, pixels + LANES), bf16),
            jax.ShapeDtypeStruct((2 * kinds, pixels), bf16),
            jax.ShapeDtypeStruct(names.shape, jnp.int32),
            jax.ShapeDtypeStruct(references.shape, bf16),
            jax.ShapeDtypeStruct(turns.shape[:2] + (LANES,), bf16),
        ],
        name="start",
        **limits(16, 1 << 20, 0),
    )(seed(), references, particles, turns, table, kind, names)


def prepare_kernel(pack, after, turns, power, matrix, response):
    turn_count, angles, _ = turns.shape
    kinds, width = power.shape[0] // 2, power.shape[1]
    tiles = width // LANES
    inside = same_cycle(angles)
    lhs = jnp.concatenate(
        [
            jnp.concatenate(
                [power[k * kinds:(k + 1) * kinds, t * LANES:(t + 1) * LANES] for k in range(2)], axis=1
            )
            for t in range(tiles)
        ],
        axis=0,
    )
    for i in range(turn_count // pack):
        wide = turn_matrix(turns, i, pack, inside)
        matrix[i * LANES:(i + 1) * LANES, :] = wide
        value = dot(lhs, jnp.concatenate([wide, wide], axis=0), NN).astype(bf16)
        for j in range(pack):
            for t in range(tiles):
                response[i * kinds:(i + 1) * kinds, j * width + t * LANES:j * width + (t + 1) * LANES] = value[
                    t * kinds:(t + 1) * kinds, j * LANES:(j + 1) * LANES
                ]


def prepare(turns, power, pack, after):
    turn_count = turns.shape[0]
    kinds, pixels = power.shape[0] // 2, power.shape[1]
    steps = turn_count // pack
    return pl.pallas_call(
        functools.partial(prepare_kernel, pack),
        in_specs=[VMEM] * 3,
        out_specs=[VMEM] * 2,
        out_shape=[
            jax.ShapeDtypeStruct((steps * LANES, pack * LANES), bf16),
            jax.ShapeDtypeStruct((steps * kinds, pack * pixels), bf16),
        ],
        name="prepare",
        **limits(16, PREPARE, 0),
    )(after, turns, power)


def rotate_kernel(groups, pack, power2, turns, *rest):
    refs = rest[:-4]
    rotated, mean, center, energy = rest[-4:]
    turn_count, angles, _ = turns.shape
    inside_cycle = same_cycle(angles)
    kinds, pixels = power2.shape[0] // 2, power2.shape[1]
    cpg = ROWS // pack
    tiles = pixels // LANES
    group_pairs = cpg * turn_count
    source = jnp.concatenate([block[...].astype(f32) for block in refs], axis=0)
    line = lax.broadcasted_iota(jnp.int32, (ROWS, pixels), 0) // cpg
    copies = []
    for i in range(groups // pack):
        tile = source[i * ROWS:(i + 1) * ROWS, :]
        for k in range(pack):
            out = tile
            for j in range(pack):
                if j != k:
                    out = jnp.where(line == j, pltpu.roll(tile, (j - k) % pack * cpg, 0), out)
            copies.append(out)
    source = jnp.concatenate(copies, axis=0)
    inside = lax.broadcasted_iota(jnp.int32, (groups * ROWS, LANES), 0) % ROWS // cpg
    lhs = jnp.concatenate(
        [
            jnp.concatenate(
                [jnp.where(inside == j, source[:, t * LANES:(t + 1) * LANES], 0.0) for j in range(pack)], axis=1
            )
            for t in range(tiles)
        ],
        axis=0,
    ).astype(bf16)
    for s in range(turn_count // (2 * pack)):
        both = [turn_matrix(turns, 2 * s + h, pack, inside_cycle) for h in range(2)]
        value = dot(lhs, jnp.concatenate(both, axis=0), NT)
        for t in range(tiles):
            for g in range(groups):
                at = (t * groups + g) * ROWS
                pair = [value[at:at + ROWS, h * LANES:(h + 1) * LANES] for h in range(2)]
                to = g * group_pairs + s * 2 * ROWS
                rotated[to:to + 2 * ROWS, t * LANES:(t + 1) * LANES] = jnp.concatenate(pair, axis=0).astype(bf16)
    power = power2[...]
    pairs = groups * group_pairs
    rows = math.gcd(pairs, 256)
    summed = jnp.zeros((kinds, 1), f32)
    for i in range(pairs // rows):
        at = slice(i * rows, (i + 1) * rows)
        value = rotated[at, :pixels].astype(f32)
        hi, lo = split(value * value, 2)
        total = dot(power, hi, NT) + dot(power, lo, NT)
        total = -0.5 * (total[:kinds] + total[kinds:])
        energy[:, at] = total
        summed = summed + jnp.sum(total, axis=1, keepdims=True)

    @pl.when(pl.program_id(0) == 0)
    def _():
        center[...] = summed * (1.0 / pairs)

    spread = lax.broadcasted_iota(jnp.int32, (kinds, LANES), 0) == lax.broadcasted_iota(jnp.int32, (kinds, LANES), 1)
    mean[...] = jnp.sum(jnp.where(spread, center[...], 0.0), axis=0, keepdims=True)
    blank = jnp.zeros((LANES - 3 * kinds, LANES), f32)
    for i in range(pairs // LANES):
        at = slice(i * LANES, (i + 1) * LANES)
        parts = [part.astype(f32) for part in split(energy[:, at] - center[...], 3)]
        rotated[at, pixels:] = jnp.concatenate(parts + [blank], axis=0).T.astype(bf16)


def rotate(refs, turns, power2, pack, groups):
    kinds, pixels = power2.shape[0] // 2, power2.shape[1]
    turn_count = turns.shape[0]
    cpg = ROWS // pack
    groups_all = sum(block.shape[0] for block in refs) // cpg
    steps = groups_all // groups
    pairs = groups * cpg * turn_count
    return pl.pallas_call(
        functools.partial(rotate_kernel, groups, pack),
        grid=(steps,),
        in_specs=[same_spec(steps, power2.shape), same_spec(steps, turns.shape)]
        + [block_spec(steps, (block.shape[0] // steps, pixels), 0) for block in refs],
        out_specs=[block_spec(steps, (pairs, pixels + LANES), 0), same_spec(steps, (1, LANES))],
        out_shape=[
            jax.ShapeDtypeStruct((steps * pairs, pixels + LANES), bf16),
            jax.ShapeDtypeStruct((1, LANES), f32),
        ],
        scratch_shapes=[pltpu.VMEM((kinds, 1), f32), pltpu.VMEM((kinds, pairs), f32)],
        name="rotate",
        **limits(12 if steps == 1 else 32, 8 * steps * pairs * pixels * 64, 2 * steps * pairs * pixels),
    )(power2, turns, *refs)


def score_kernel(groups, scale, begin, me, here, weighted, names, rotated, *rest):
    outs, acc = rest[:-1], rest[-1]
    step = pl.program_id(0)
    count = acc.shape[1]
    pairs = rotated.shape[0] // groups
    span = math.gcd(count, 256)
    for n in range(count // span):
        cols = slice(n * span, (n + 1) * span)
        at = slice(begin + n * span, begin + (n + 1) * span)
        pix = weighted[at, :]
        for g in range(groups):
            value = scale * dot(rotated[g * pairs:(g + 1) * pairs, :], pix, NT)
            group = group_at(step * groups + g, here)
            for k in range(2):
                rows = slice(k * pairs, (k + 1) * pairs)
                hit = names[k:k + 1, at] == group
                if g == 0:
                    hit = hit | (step == 0)
                acc[rows, cols] = jnp.where(hit, value, acc[rows, cols])

    @pl.when(step == pl.num_programs(0) - 1)
    def _():
        share = outs[0].shape[1]
        for k, out in enumerate(outs):
            start = pl.multiple_of((me[0] ^ k) * share, share)
            out[...] = acc[:, pl.ds(start, share)]


def score(begin, count, weighted, names, rotated, me, here, peers, group_pairs, groups, scale):
    width = weighted.shape[1]
    steps = rotated.shape[0] // (group_pairs * groups)
    share = count // peers
    rows = 2 * group_pairs
    return pl.pallas_call(
        functools.partial(score_kernel, groups, scale, begin),
        grid=(steps,),
        in_specs=[
            SMEM,
            SMEM,
            same_spec(steps, weighted.shape),
            same_spec(steps, names.shape),
            block_spec(steps, (groups * group_pairs, width), 0),
        ],
        out_specs=[same_spec(steps, (rows, share))] * peers,
        out_shape=[jax.ShapeDtypeStruct((rows, share), f32)] * peers,
        scratch_shapes=[pltpu.VMEM((rows, count), f32)],
        name="score",
        **limits(12 if steps == 1 else 32, 2 * rotated.shape[0] * width * count, 2 * rotated.shape[0] * width),
    )(me, here, weighted, names, rotated)


def soften_kernel(scores, mean, out):
    value = scores[...]
    rows, share = value.shape
    top = jnp.max(value, axis=0, keepdims=True)
    grown = jnp.exp(value - top)
    total = jnp.sum(grown, axis=0, keepdims=True)
    out[:rows, :] = (grown * (1.0 / total)).astype(bf16)
    tail = jnp.zeros((2 * ROWS, share), f32)
    at = lax.broadcasted_iota(jnp.int32, tail.shape, 0)
    centers = mean[...]
    if share > LANES:
        centers = jnp.concatenate([centers, jnp.zeros((1, share - LANES), f32)], axis=1)
    for i, row in enumerate(split(top + jnp.log(total), 3) + split(centers, 3)):
        tail = jnp.where(at == i, row.astype(f32), tail)
    out[rows:, :] = tail.astype(bf16)


def soften(scores, mean):
    rows, share = scores.shape
    return pl.pallas_call(
        soften_kernel,
        in_specs=[VMEM, VMEM],
        out_specs=VMEM,
        out_shape=jax.ShapeDtypeStruct((rows + 2 * ROWS, share), bf16),
        name="soften",
        **limits(8, 4 * rows * share, 6 * rows * share, rows * share),
    )(scores, mean)


def collect_kernel(groups, parts, turn_count, kinds, scale, begin, peers, first, last, me, here, names, weighted, *rest):
    rest = list(rest)
    take = lambda n: [rest.pop(0) for _ in range(n)]
    matrix, response = take(2) if last else (None, None)
    blocks = take(peers)
    before = None if first else take(3)
    sums = take(parts) if last else None
    logs, weights, lhs, by_kind = rest if last else [rest[i] for i in (2, 3, 0, 1)]
    step = pl.program_id(0)
    pixels = weighted.shape[1] - LANES
    share = blocks[0].shape[1]
    count = share * peers
    rows = weights.shape[0]
    pairs = rows // 2
    turns = lhs.shape[1] // LANES
    pack = turn_count // turns
    cpg = ROWS // pack
    tiles = pixels // LANES
    own = slice(begin, begin + count)

    @pl.when(step == 0)
    def _():
        center = jnp.zeros((1, share), f32)
        for k, block in enumerate(blocks):
            start = pl.multiple_of((me[0] ^ k) * share, share)
            weights[:, pl.ds(start, share)] = block[:rows, :]
            tail = block[rows:, :].astype(f32)
            logs[0:1, pl.ds(begin + start, share)] = tail[0:1] + tail[1:2] + tail[2:3]
            center = center + (tail[3:4] + tail[4:5] + tail[5:6])
        line = lax.broadcasted_iota(jnp.int32, (2 * ROWS, LANES), 0)
        inside = lax.broadcasted_iota(jnp.int32, (2 * ROWS, LANES), 1) < kinds
        stacked = jnp.zeros((2 * ROWS, LANES), f32)
        for i, part in enumerate(split(center[:, :LANES], 3)):
            stacked = jnp.where((line == i) & inside, part.astype(f32), stacked)
        moved = dot(stacked.astype(bf16), weighted[own, pixels:], NT)
        logs[:, own] = logs[:, own] + scale * jnp.sum(moved, axis=0, keepdims=True)
        if not first:
            logs[:, :begin] = before[2][:, :begin]

    zero = jnp.zeros((), bf16)
    for g in range(0, groups, 2):
        dense = []
        for q in range(2):
            group = group_at(step * groups + g + q, here)
            dense.append(
                jnp.where(names[0:1, own] == group, weights[:pairs, :], zero)
                + jnp.where(names[1:2, own] == group, weights[pairs:, :], zero)
            )
        value = dot(jnp.concatenate(dense, axis=0), weighted[own, :], NN)
        for i in range(turns):
            lanes = slice(i * LANES, (i + 1) * LANES)
            for t in range(tiles):
                pair = [
                    value[q * pairs + i * ROWS:q * pairs + (i + 1) * ROWS, t * LANES:(t + 1) * LANES]
                    for q in range(2)
                ]
                pair = jnp.concatenate(pair, axis=0)
                at = slice((t * groups + g) * ROWS, (t * groups + g + 2) * ROWS)
                if not first:
                    pair = pair + before[0][at, lanes]
                lhs[at, lanes] = pair.astype(lhs.dtype)
            for q in range(2):
                by_kind[(g + q) * ROWS:(g + q + 1) * ROWS, i * kinds:(i + 1) * kinds] = value[
                    q * pairs + i * ROWS:q * pairs + (i + 1) * ROWS, pixels:pixels + kinds
                ]
    if not last:
        if not first:
            by_kind[...] = by_kind[...] + before[1][...]
        return
    total = dot(lhs[...], matrix[...], NN)
    light = by_kind[...] if first else by_kind[...] + before[1][...]
    heavy = dot(jnp.concatenate(split(light, 2), axis=0), response[...], NN)
    heavy = heavy[:groups * ROWS] + heavy[groups * ROWS:]
    upper = lax.broadcasted_iota(jnp.int32, (ROWS, LANES), 0) < cpg

    def fold(terms):
        out = terms[0]
        for j in range(1, pack):
            out = out + pltpu.roll(terms[j], ROWS - j * cpg, 0)
        return out

    for g in range(groups):
        part, to = g % parts, slice(g // parts * ROWS, (g // parts + 1) * ROWS)
        for t in range(tiles):
            lanes = slice(t * LANES, (t + 1) * LANES)
            at = slice((t * groups + g) * ROWS, (t * groups + g + 1) * ROWS)
            top = fold([total[at, j * LANES:(j + 1) * LANES] for j in range(pack)])
            at = slice(g * ROWS, (g + 1) * ROWS)
            low = fold(
                [heavy[at, j * pixels + t * LANES:j * pixels + (t + 1) * LANES] for j in range(pack)]
            )
            sums[part][to, lanes] = jnp.where(upper, top, pltpu.roll(low, cpg, 0))


def collect(
    begin, blocks, before, last, names, weighted, matrix, response, me, here, parts, turn_count, kinds, group_pairs,
    groups, groups_all, scale
):
    count, width = weighted.shape
    pixels = width - LANES
    peers = len(blocks)
    steps = groups_all // groups
    turns = matrix.shape[0] // LANES
    rows = groups * ROWS // parts
    first = not before
    left = (pixels // LANES * groups * ROWS, turns * LANES)
    light = (groups * ROWS, turns * kinds)
    logs_spec = same_spec(steps, (1, count))
    logs_shape = jax.ShapeDtypeStruct((1, count), f32)
    sides = [block_spec(steps, left, 0), block_spec(steps, light, 0)]
    weights_scratch = pltpu.VMEM((2 * group_pairs, peers * blocks[0].shape[1]), bf16)
    if last:
        out_specs = [block_spec(steps, (rows, pixels), 0)] * parts + [logs_spec]
        out_shape = [jax.ShapeDtypeStruct((steps * rows, pixels), f32)] * parts + [logs_shape]
        scratch = [weights_scratch, pltpu.VMEM(left, bf16), pltpu.VMEM(light, f32)]
    else:
        out_specs = sides + [logs_spec]
        out_shape = [jax.ShapeDtypeStruct((steps * shape[0], shape[1]), f32) for shape in (left, light)] + [logs_shape]
        scratch = [weights_scratch]
    both = [names, weighted] + ([matrix, response] if last else []) + blocks
    return pl.pallas_call(
        functools.partial(
            collect_kernel, groups, parts, turn_count, kinds, scale, begin, peers, first, last
        ),
        grid=(steps,),
        in_specs=[SMEM, SMEM]
        + [same_spec(steps, a.shape) for a in both]
        + ([] if first else sides + [logs_spec]),
        out_specs=out_specs,
        out_shape=out_shape,
        scratch_shapes=scratch,
        name="collect",
        **limits(
            20 if steps == 1 else 56, 2 * groups_all * group_pairs * width * peers * blocks[0].shape[1],
            4 * count * pixels
        ),
    )(me, here, *both, *before)


def add_kernel(left, right, *outs):
    rows = outs[0].shape[0]
    for i, out in enumerate(outs):
        at = slice(i * rows, (i + 1) * rows)
        out[...] = left[at, :] + right[at, :]


def add_cut(left, right, pieces):
    shape = (left.shape[0] // pieces, left.shape[1])
    return pl.pallas_call(
        add_kernel,
        in_specs=[VMEM, VMEM],
        out_specs=[VMEM] * pieces,
        out_shape=[jax.ShapeDtypeStruct(shape, f32)] * pieces,
        name="add_cut",
        **limits(4, left.size, 12 * left.size),
    )(left, right)


def finish_kernel(*refs):
    sums, weights = refs[-2:]
    total = refs[0][...]
    for ref in refs[1:-2]:
        total = total + ref[...]
    sums[...] = total[:sums.shape[0], :].astype(bf16)
    weights[...] = total[sums.shape[0]:, :]


def finish(pieces, cpg):
    shape = (cpg, pieces[0].shape[1])
    return pl.pallas_call(
        finish_kernel,
        in_specs=[VMEM] * len(pieces),
        out_specs=[VMEM] * 2,
        out_shape=[jax.ShapeDtypeStruct(shape, bf16), jax.ShapeDtypeStruct(shape, f32)],
        name="finish",
        **limits(4, pieces[0].size, 12 * pieces[0].size),
    )(*pieces)


def swap(x, axis, k):
    return lax.ppermute(x, axis, [(i, i ^ k) for i in range(lax.axis_size(axis))])


def local(particles, candidates, defocus, ctf_table, references, rotations):
    count, pixels = particles.shape
    peers = lax.axis_size("cls")
    owners = lax.axis_size("dom")
    paired = owners & (owners - 1) == 0 and 4 <= owners <= 8
    turn_count = rotations.shape[0]
    cpg = references.shape[0]
    pack = ROWS // cpg
    group_pairs = cpg * turn_count
    groups = math.gcd(owners, 8)
    kinds = ctf_table.shape[0]
    scale = 4.0 / math.sqrt(pixels * peers)
    me = lax.axis_index("cls").astype(jnp.int32).reshape(1)
    here = (lax.axis_index("dom") if paired else jnp.int32(0)).astype(jnp.int32).reshape(1)
    weighted, power2, names, own_refs, turns2 = start(
        particles, references, rotations, ctf_table, defocus.reshape(1, count), candidates.T
    )
    if paired:
        line = [own_refs] + [swap(references, "dom", 2 * k) for k in range(1, owners // 2)]
        refs = [half for block in line for half in (block, swap(references if block is own_refs else block, "dom", 1))]
    else:
        refs = [lax.all_gather(references, "dom", axis=0, tiled=True)]
    rotated, mean = rotate(refs, turns2, power2, pack, groups)
    chunks = 2
    size = count // chunks
    blocks = []
    for c in range(chunks):
        cut = score(c * size, size, weighted, names, rotated, me, here, peers, group_pairs, groups, scale)
        total = cut[0]
        for k in range(1, peers):
            total = total + swap(cut[k].astype(jnp.float16), "cls", k).astype(f32)
        own = soften(total, mean)
        blocks.append([own] + [swap(own, "cls", k) for k in range(1, peers)])
    matrix, response = prepare(turns2, power2, pack, blocks[0][0])
    parts = 2 if paired else 1
    out = []
    for c in range(chunks):
        out = collect(
            c * size, blocks[c], out, c == chunks - 1, names, weighted, matrix, response, me, here, parts, turn_count,
            kinds, group_pairs, groups, owners, scale
        )
    if paired:
        pieces = add_cut(out[0], swap(out[1], "dom", 1), owners // 2)
        pieces = [pieces[0]] + [swap(pieces[k], "dom", 2 * k) for k in range(1, owners // 2)]
    else:
        pieces = [lax.psum_scatter(out[0], "dom", scatter_dimension=0, tiled=True)]
    class_sums, class_weights = finish(pieces, cpg)
    return class_sums, class_weights, out[-1].reshape(count)


def solution(mesh):
    in_specs = (P("dom", "cls"), P("dom", None), P("dom"), P(None, "cls"), P("dom", "cls"), P())
    out_specs = (P("dom", "cls"), P("dom", "cls"), P("dom"))
    return jax.shard_map(local, mesh=mesh, in_specs=in_specs, out_specs=out_specs, check_vma=False)
```

```python
import functools
import math

import jax
import jax.numpy as jnp
from jax import lax
from jax.experimental import pallas as pl
from jax.experimental.pallas import tpu as pltpu
from jax.sharding import PartitionSpec as P

f32, bf16 = jnp.float32, jnp.bfloat16
VMEM = pl.BlockSpec(memory_space=pltpu.VMEM)
SMEM = pl.BlockSpec(memory_space=pltpu.SMEM)
LANES, ROWS = 128, 8
PREPARE = 4_000_000_000
EARLY = 20_000_000_000
NN = (((1,), (0,)), ((), ()))
NT = (((1,), (1,)), ((), ()))


def dot(a, b, dims):
    return lax.dot_general(a, b, dims, preferred_element_type=f32)


def split(x, parts):
    out = []
    for _ in range(parts):
        out.append(x.astype(bf16))
        x = x - out[-1].astype(f32)
    return out


def limits(mib, flops, moved, transcendentals=0):
    return dict(
        compiler_params=pltpu.CompilerParams(vmem_limit_bytes=mib << 20),
        cost_estimate=pl.CostEstimate(flops=flops, bytes_accessed=moved, transcendentals=transcendentals),
    )


def group_at(place, here):
    return place ^ here[0]


def block_spec(steps, shape, dim):
    if steps == 1:
        return VMEM
    index = lambda i: tuple(i if d == dim else 0 for d in range(len(shape)))
    return pl.BlockSpec(shape, index)


def same_spec(steps, shape):
    return VMEM if steps == 1 else pl.BlockSpec(shape, lambda i: (0,) * len(shape))


def turn_matrix(turns, i, pack, inside):
    _, angles, width = turns.shape
    per = LANES // angles
    wide = []
    for j in range(pack):
        turn = turns[i * pack + j]
        turn = jnp.concatenate([jnp.concatenate([turn] * (LANES // width), axis=1)] * per, axis=0)
        wide.append(jnp.where(inside, turn, jnp.zeros((), bf16)))
    return jnp.concatenate(wide, axis=1)


def same_cycle(angles):
    row = lax.broadcasted_iota(jnp.int32, (LANES, LANES), 0) // angles
    col = lax.broadcasted_iota(jnp.int32, (LANES, LANES), 1) // angles
    return row == col


def seed_kernel(out):
    out[...] = lax.broadcasted_iota(jnp.int32, out.shape, 0)


def seed():
    return pl.pallas_call(
        seed_kernel,
        out_specs=VMEM,
        out_shape=jax.ShapeDtypeStruct((LANES, 2 * LANES), jnp.int32),
        name="seed",
        **limits(4, EARLY, 0),
    )()


def start_kernel(numbers, own_in, pixels, turns, table, kind, names_in, weighted, power, names, own, turns2):
    names[...] = names_in[...]
    own[...] = own_in[...]
    for i in range(turns.shape[0]):
        turns2[i] = jnp.concatenate([turns[i]] * (LANES // turns.shape[2]), axis=1)
    kinds, width = table.shape
    power[...] = jnp.concatenate(split(table[...] * table[...], 2), axis=0)
    table3 = jnp.concatenate(split(table[...], 3), axis=0)
    count = pixels.shape[0]
    rows = math.gcd(count, 256)
    ids = numbers[:, :rows]
    for i in range(count // rows):
        at = slice(i * rows, (i + 1) * rows)
        hit = jnp.where((ids % kinds == kind[:, at]) & (ids < 3 * kinds), 1.0, 0.0).T.astype(bf16)
        factor = dot(hit[:, :3 * kinds], table3, NN)
        weighted[at, :width] = (pixels[at, :].astype(f32) * factor).astype(bf16)
        weighted[at, width:] = hit


def start(particles, references, turns, table, kind, names):
    count, pixels = particles.shape
    kinds = table.shape[0]
    return pl.pallas_call(
        start_kernel,
        in_specs=[VMEM] * 7,
        out_specs=[VMEM] * 5,
        out_shape=[
            jax.ShapeDtypeStruct((count, pixels + LANES), bf16),
            jax.ShapeDtypeStruct((2 * kinds, pixels), bf16),
            jax.ShapeDtypeStruct(names.shape, jnp.int32),
            jax.ShapeDtypeStruct(references.shape, bf16),
            jax.ShapeDtypeStruct(turns.shape[:2] + (LANES,), bf16),
        ],
        name="start",
        **limits(16, 1 << 20, 0),
    )(seed(), references, particles, turns, table, kind, names)


def prepare_kernel(pack, after, turns, power, matrix, response, sign):
    sign[...] = jnp.zeros_like(sign)
    turn_count, angles, _ = turns.shape
    kinds, width = power.shape[0] // 2, power.shape[1]
    tiles = width // LANES
    inside = same_cycle(angles)
    lhs = jnp.concatenate(
        [
            jnp.concatenate(
                [power[k * kinds:(k + 1) * kinds, t * LANES:(t + 1) * LANES] for k in range(2)], axis=1
            )
            for t in range(tiles)
        ],
        axis=0,
    )
    for i in range(turn_count // pack):
        wide = turn_matrix(turns, i, pack, inside)
        matrix[i * LANES:(i + 1) * LANES, :] = wide
        value = dot(lhs, jnp.concatenate([wide, wide], axis=0), NN).astype(bf16)
        for j in range(pack):
            for t in range(tiles):
                response[i * kinds:(i + 1) * kinds, j * width + t * LANES:j * width + (t + 1) * LANES] = value[
                    t * kinds:(t + 1) * kinds, j * LANES:(j + 1) * LANES
                ]


def prepare(turns, power, pack, after):
    turn_count = turns.shape[0]
    kinds, pixels = power.shape[0] // 2, power.shape[1]
    steps = turn_count // pack
    return pl.pallas_call(
        functools.partial(prepare_kernel, pack),
        in_specs=[VMEM] * 3,
        out_specs=[VMEM] * 3,
        out_shape=[
            jax.ShapeDtypeStruct((steps * LANES, pack * LANES), bf16),
            jax.ShapeDtypeStruct((steps * kinds, pack * pixels), bf16),
            jax.ShapeDtypeStruct((ROWS, LANES), f32),
        ],
        name="prepare",
        **limits(16, PREPARE, 0),
    )(after, turns, power)


def rotate_kernel(groups, pack, power2, turns, *rest):
    refs = rest[:-4]
    rotated, mean, center, energy = rest[-4:]
    turn_count, angles, _ = turns.shape
    inside_cycle = same_cycle(angles)
    kinds, pixels = power2.shape[0] // 2, power2.shape[1]
    cpg = ROWS // pack
    tiles = pixels // LANES
    group_pairs = cpg * turn_count
    source = jnp.concatenate([block[...].astype(f32) for block in refs], axis=0)
    line = lax.broadcasted_iota(jnp.int32, (ROWS, pixels), 0) // cpg
    copies = []
    for i in range(groups // pack):
        tile = source[i * ROWS:(i + 1) * ROWS, :]
        for k in range(pack):
            out = tile
            for j in range(pack):
                if j != k:
                    out = jnp.where(line == j, pltpu.roll(tile, (j - k) % pack * cpg, 0), out)
            copies.append(out)
    source = jnp.concatenate(copies, axis=0)
    inside = lax.broadcasted_iota(jnp.int32, (groups * ROWS, LANES), 0) % ROWS // cpg
    lhs = jnp.concatenate(
        [
            jnp.concatenate(
                [jnp.where(inside == j, source[:, t * LANES:(t + 1) * LANES], 0.0) for j in range(pack)], axis=1
            )
            for t in range(tiles)
        ],
        axis=0,
    ).astype(bf16)
    for s in range(turn_count // (2 * pack)):
        both = [turn_matrix(turns, 2 * s + h, pack, inside_cycle) for h in range(2)]
        value = dot(lhs, jnp.concatenate(both, axis=0), NT)
        for t in range(tiles):
            for g in range(groups):
                at = (t * groups + g) * ROWS
                pair = [value[at:at + ROWS, h * LANES:(h + 1) * LANES] for h in range(2)]
                to = g * group_pairs + s * 2 * ROWS
                rotated[to:to + 2 * ROWS, t * LANES:(t + 1) * LANES] = jnp.concatenate(pair, axis=0).astype(bf16)
    power = power2[...]
    pairs = groups * group_pairs
    rows = math.gcd(pairs, 256)
    summed = jnp.zeros((kinds, 1), f32)
    for i in range(pairs // rows):
        at = slice(i * rows, (i + 1) * rows)
        value = rotated[at, :pixels].astype(f32)
        hi, lo = split(value * value, 2)
        total = dot(power, hi, NT) + dot(power, lo, NT)
        total = -0.5 * (total[:kinds] + total[kinds:])
        energy[:, at] = total
        summed = summed + jnp.sum(total, axis=1, keepdims=True)

    @pl.when(pl.program_id(0) == 0)
    def _():
        center[...] = summed * (1.0 / pairs)

    spread = lax.broadcasted_iota(jnp.int32, (kinds, LANES), 0) == lax.broadcasted_iota(jnp.int32, (kinds, LANES), 1)
    mean[...] = jnp.sum(jnp.where(spread, center[...], 0.0), axis=0, keepdims=True)
    blank = jnp.zeros((LANES, LANES - 2 * kinds), bf16)
    for i in range(pairs // LANES):
        at = slice(i * LANES, (i + 1) * LANES)
        parts = jnp.concatenate(split(energy[:, at] - center[...], 2), axis=0).T
        rotated[at, pixels:] = jnp.concatenate([parts, blank], axis=1)


def rotate(refs, turns, power2, pack, groups):
    kinds, pixels = power2.shape[0] // 2, power2.shape[1]
    turn_count = turns.shape[0]
    cpg = ROWS // pack
    groups_all = sum(block.shape[0] for block in refs) // cpg
    steps = groups_all // groups
    pairs = groups * cpg * turn_count
    return pl.pallas_call(
        functools.partial(rotate_kernel, groups, pack),
        grid=(steps,),
        in_specs=[same_spec(steps, power2.shape), same_spec(steps, turns.shape)]
        + [block_spec(steps, (block.shape[0] // steps, pixels), 0) for block in refs],
        out_specs=[block_spec(steps, (pairs, pixels + LANES), 0), same_spec(steps, (1, LANES))],
        out_shape=[
            jax.ShapeDtypeStruct((steps * pairs, pixels + LANES), bf16),
            jax.ShapeDtypeStruct((1, LANES), f32),
        ],
        scratch_shapes=[pltpu.VMEM((kinds, 1), f32), pltpu.VMEM((kinds, pairs), f32)],
        name="rotate",
        **limits(12 if steps == 1 else 32, 8 * steps * pairs * pixels * 64, 2 * steps * pairs * pixels),
    )(power2, turns, *refs)


def score_kernel(groups, scale, begin, me, here, weighted, names, rotated, *rest):
    outs, acc = rest[:-1], rest[-1]
    step = pl.program_id(0)
    count = acc.shape[1]
    pairs = rotated.shape[0] // groups
    span = math.gcd(count, 256)
    for n in range(count // span):
        cols = slice(n * span, (n + 1) * span)
        at = slice(begin + n * span, begin + (n + 1) * span)
        pix = weighted[at, :]
        for g in range(groups):
            value = scale * dot(rotated[g * pairs:(g + 1) * pairs, :], pix, NT)
            group = group_at(step * groups + g, here)
            for k in range(2):
                rows = slice(k * pairs, (k + 1) * pairs)
                hit = names[k:k + 1, at] == group
                if g == 0:
                    hit = hit | (step == 0)
                acc[rows, cols] = jnp.where(hit, value, acc[rows, cols])

    @pl.when(step == pl.num_programs(0) - 1)
    def _():
        share = outs[0].shape[1]
        for k, out in enumerate(outs):
            start = pl.multiple_of((me[0] ^ k) * share, share)
            out[...] = acc[:, pl.ds(start, share)]


def score(begin, count, weighted, names, rotated, me, here, peers, group_pairs, groups, scale):
    width = weighted.shape[1]
    steps = rotated.shape[0] // (group_pairs * groups)
    share = count // peers
    rows = 2 * group_pairs
    return pl.pallas_call(
        functools.partial(score_kernel, groups, scale, begin),
        grid=(steps,),
        in_specs=[
            SMEM,
            SMEM,
            same_spec(steps, weighted.shape),
            same_spec(steps, names.shape),
            block_spec(steps, (groups * group_pairs, width), 0),
        ],
        out_specs=[same_spec(steps, (rows, share))] * peers,
        out_shape=[jax.ShapeDtypeStruct((rows, share), f32)] * peers,
        scratch_shapes=[pltpu.VMEM((rows, count), f32)],
        name="score",
        **limits(12 if steps == 1 else 32, 2 * rotated.shape[0] * width * count, 2 * rotated.shape[0] * width),
    )(me, here, weighted, names, rotated)


def soften_kernel(scores, mean, *rest):
    out = rest[-1]
    value = scores[...]
    rows, share = value.shape
    top = jnp.max(value, axis=0, keepdims=True)
    grown = jnp.exp(value - top)
    total = jnp.sum(grown, axis=0, keepdims=True)
    out[:rows, :] = (grown * (1.0 / total)).astype(bf16)
    tail = jnp.zeros((2 * ROWS, share), f32)
    at = lax.broadcasted_iota(jnp.int32, tail.shape, 0)
    centers = mean[...]
    if share > LANES:
        centers = jnp.concatenate([centers, jnp.zeros((1, share - LANES), f32)], axis=1)
    for i, row in enumerate(split(top + jnp.log(total), 3) + split(centers, 3)):
        tail = jnp.where(at == i, row.astype(f32), tail)
    out[rows:, :] = tail.astype(bf16)


def soften(scores, mean, *after):
    rows, share = scores.shape
    return pl.pallas_call(
        soften_kernel,
        in_specs=[VMEM] * (2 + len(after)),
        out_specs=VMEM,
        out_shape=jax.ShapeDtypeStruct((rows + 2 * ROWS, share), bf16),
        name="soften",
        **limits(8, 4 * rows * share, 6 * rows * share, rows * share),
    )(scores, mean, *after)


def collect_kernel(groups, parts, turn_count, kinds, scale, begin, peers, first, last, me, here, names, weighted, *rest):
    rest = list(rest)
    take = lambda n: [rest.pop(0) for _ in range(n)]
    matrix, response = take(2) if last else (None, None)
    blocks = take(peers)
    before = None if first else take(3)
    sums = take(parts) if last else None
    logs, weights, lhs, by_kind = rest if last else [rest[i] for i in (2, 3, 0, 1)]
    step = pl.program_id(0)
    pixels = weighted.shape[1] - LANES
    share = blocks[0].shape[1]
    count = share * peers
    rows = weights.shape[0]
    pairs = rows // 2
    turns = lhs.shape[1] // LANES
    pack = turn_count // turns
    cpg = ROWS // pack
    tiles = pixels // LANES
    own = slice(begin, begin + count)

    @pl.when(step == 0)
    def _():
        center = jnp.zeros((1, share), f32)
        for k, block in enumerate(blocks):
            start = pl.multiple_of((me[0] ^ k) * share, share)
            weights[:, pl.ds(start, share)] = block[:rows, :]
            tail = block[rows:, :].astype(f32)
            logs[0:1, pl.ds(begin + start, share)] = tail[0:1] + tail[1:2] + tail[2:3]
            center = center + (tail[3:4] + tail[4:5] + tail[5:6])
        line = lax.broadcasted_iota(jnp.int32, (2 * ROWS, LANES), 0)
        inside = lax.broadcasted_iota(jnp.int32, (2 * ROWS, LANES), 1) < kinds
        stacked = jnp.zeros((2 * ROWS, LANES), f32)
        for i, part in enumerate(split(center[:, :LANES], 3)):
            stacked = jnp.where((line == i) & inside, part.astype(f32), stacked)
        moved = dot(stacked.astype(bf16), weighted[own, pixels:], NT)
        logs[:, own] = logs[:, own] + scale * jnp.sum(moved, axis=0, keepdims=True)
        if not first:
            logs[:, :begin] = before[2][:, :begin]

    halves = 2 if groups % 4 == 0 else 1
    span = groups // halves
    row_of = lambda t, g: ((g // span * tiles + t) * span + g % span) * ROWS
    totals = []
    zero = jnp.zeros((), bf16)
    for g in range(0, groups, 2):
        dense = []
        for q in range(2):
            group = group_at(step * groups + g + q, here)
            dense.append(
                jnp.where(names[0:1, own] == group, weights[:pairs, :], zero)
                + jnp.where(names[1:2, own] == group, weights[pairs:, :], zero)
            )
        value = dot(jnp.concatenate(dense, axis=0), weighted[own, :], NN)
        for i in range(turns):
            lanes = slice(i * LANES, (i + 1) * LANES)
            for t in range(tiles):
                pair = [
                    value[q * pairs + i * ROWS:q * pairs + (i + 1) * ROWS, t * LANES:(t + 1) * LANES]
                    for q in range(2)
                ]
                pair = jnp.concatenate(pair, axis=0)
                at = slice(row_of(t, g), row_of(t, g) + 2 * ROWS)
                if not first:
                    pair = pair + before[0][at, lanes]
                lhs[at, lanes] = pair.astype(lhs.dtype)
            for q in range(2):
                by_kind[(g + q) * ROWS:(g + q + 1) * ROWS, i * kinds:(i + 1) * kinds] = value[
                    q * pairs + i * ROWS:q * pairs + (i + 1) * ROWS, pixels:pixels + kinds
                ]
        if last and (g + 2) % span == 0:
            at = slice(len(totals) * tiles * span * ROWS, (len(totals) + 1) * tiles * span * ROWS)
            totals.append(dot(lhs[at, :], matrix[...], NN))
    if not last:
        if not first:
            by_kind[...] = by_kind[...] + before[1][...]
        return
    light = by_kind[...] if first else by_kind[...] + before[1][...]
    heavy = dot(jnp.concatenate(split(light, 2), axis=0), response[...], NN)
    heavy = heavy[:groups * ROWS] + heavy[groups * ROWS:]
    upper = lax.broadcasted_iota(jnp.int32, (ROWS, LANES), 0) < cpg

    def fold(terms):
        out = terms[0]
        for j in range(1, pack):
            out = out + pltpu.roll(terms[j], ROWS - j * cpg, 0)
        return out

    for g in range(groups):
        part, to = g % parts, slice(g // parts * ROWS, (g // parts + 1) * ROWS)
        for t in range(tiles):
            lanes = slice(t * LANES, (t + 1) * LANES)
            at = slice((t * span + g % span) * ROWS, (t * span + g % span + 1) * ROWS)
            top = fold([totals[g // span][at, j * LANES:(j + 1) * LANES] for j in range(pack)])
            at = slice(g * ROWS, (g + 1) * ROWS)
            low = fold(
                [heavy[at, j * pixels + t * LANES:j * pixels + (t + 1) * LANES] for j in range(pack)]
            )
            sums[part][to, lanes] = jnp.where(upper, top, pltpu.roll(low, cpg, 0))


def collect(
    begin, blocks, before, last, names, weighted, matrix, response, me, here, parts, turn_count, kinds, group_pairs,
    groups, groups_all, scale
):
    count, width = weighted.shape
    pixels = width - LANES
    peers = len(blocks)
    steps = groups_all // groups
    turns = matrix.shape[0] // LANES
    rows = groups * ROWS // parts
    first = not before
    left = (pixels // LANES * groups * ROWS, turns * LANES)
    light = (groups * ROWS, turns * kinds)
    logs_spec = same_spec(steps, (1, count))
    logs_shape = jax.ShapeDtypeStruct((1, count), f32)
    sides = [block_spec(steps, left, 0), block_spec(steps, light, 0)]
    weights_scratch = pltpu.VMEM((2 * group_pairs, peers * blocks[0].shape[1]), bf16)
    if last:
        out_specs = [block_spec(steps, (rows, pixels), 0)] * parts + [logs_spec]
        out_shape = [jax.ShapeDtypeStruct((steps * rows, pixels), f32)] * parts + [logs_shape]
        scratch = [weights_scratch, pltpu.VMEM(left, bf16), pltpu.VMEM(light, f32)]
    else:
        out_specs = sides + [logs_spec]
        out_shape = [jax.ShapeDtypeStruct((steps * shape[0], shape[1]), f32) for shape in (left, light)] + [logs_shape]
        scratch = [weights_scratch]
    both = [names, weighted] + ([matrix, response] if last else []) + blocks
    return pl.pallas_call(
        functools.partial(
            collect_kernel, groups, parts, turn_count, kinds, scale, begin, peers, first, last
        ),
        grid=(steps,),
        in_specs=[SMEM, SMEM]
        + [same_spec(steps, a.shape) for a in both]
        + ([] if first else sides + [logs_spec]),
        out_specs=out_specs,
        out_shape=out_shape,
        scratch_shapes=scratch,
        name="collect",
        **limits(
            20 if steps == 1 else 56, 2 * groups_all * group_pairs * width * peers * blocks[0].shape[1],
            4 * count * pixels
        ),
    )(me, here, *both, *before)


def add_kernel(left, right, *outs):
    rows = outs[0].shape[0]
    for i, out in enumerate(outs):
        at = slice(i * rows, (i + 1) * rows)
        out[...] = left[at, :] + right[at, :]


def add_cut(left, right, pieces):
    shape = (left.shape[0] // pieces, left.shape[1])
    return pl.pallas_call(
        add_kernel,
        in_specs=[VMEM, VMEM],
        out_specs=[VMEM] * pieces,
        out_shape=[jax.ShapeDtypeStruct(shape, f32)] * pieces,
        name="add_cut",
        **limits(4, left.size, 12 * left.size),
    )(left, right)


def finish_kernel(*refs):
    sums, weights = refs[-2:]
    total = refs[0][...]
    for ref in refs[1:-2]:
        total = total + ref[...]
    sums[...] = total[:sums.shape[0], :].astype(bf16)
    weights[...] = total[sums.shape[0]:, :]


def finish(pieces, cpg):
    shape = (cpg, pieces[0].shape[1])
    return pl.pallas_call(
        finish_kernel,
        in_specs=[VMEM] * len(pieces),
        out_specs=[VMEM] * 2,
        out_shape=[jax.ShapeDtypeStruct(shape, bf16), jax.ShapeDtypeStruct(shape, f32)],
        name="finish",
        **limits(4, pieces[0].size, 12 * pieces[0].size),
    )(*pieces)


def swap(x, axis, k):
    return lax.ppermute(x, axis, [(i, i ^ k) for i in range(lax.axis_size(axis))])


def local(particles, candidates, defocus, ctf_table, references, rotations):
    count, pixels = particles.shape
    peers = lax.axis_size("cls")
    owners = lax.axis_size("dom")
    paired = owners & (owners - 1) == 0 and 4 <= owners <= 8
    turn_count = rotations.shape[0]
    cpg = references.shape[0]
    pack = ROWS // cpg
    group_pairs = cpg * turn_count
    groups = math.gcd(owners, 8)
    kinds = ctf_table.shape[0]
    scale = 4.0 / math.sqrt(pixels * peers)
    me = lax.axis_index("cls").astype(jnp.int32).reshape(1)
    here = (lax.axis_index("dom") if paired else jnp.int32(0)).astype(jnp.int32).reshape(1)
    weighted, power2, names, own_refs, turns2 = start(
        particles, references, rotations, ctf_table, defocus.reshape(1, count), candidates.T
    )
    if paired:
        line = [own_refs] + [swap(references, "dom", 2 * k) for k in range(1, owners // 2)]
        refs = [half for block in line for half in (block, swap(references if block is own_refs else block, "dom", 1))]
    else:
        refs = [lax.all_gather(references, "dom", axis=0, tiled=True)]
    rotated, mean = rotate(refs, turns2, power2, pack, groups)
    chunks = 2
    size = count // chunks
    blocks, signs = [], []
    for c in range(chunks):
        cut = score(c * size, size, weighted, names, rotated, me, here, peers, group_pairs, groups, scale)
        total = cut[0]
        for k in range(1, peers):
            total = total + swap(cut[k].astype(jnp.float16), "cls", k).astype(f32)
        own = soften(total, mean, *signs)
        if c == 0:
            matrix, response, *signs = prepare(turns2, power2, pack, own)
        blocks.append([own] + [swap(own, "cls", k) for k in range(1, peers)])
    parts = 2 if paired else 1
    out = []
    for c in range(chunks):
        out = collect(
            c * size, blocks[c], out, c == chunks - 1, names, weighted, matrix, response, me, here, parts, turn_count,
            kinds, group_pairs, groups, owners, scale
        )
    if paired:
        pieces = add_cut(out[0], swap(out[1], "dom", 1), owners // 2)
        pieces = [pieces[0]] + [swap(pieces[k], "dom", 2 * k) for k in range(1, owners // 2)]
    else:
        pieces = [lax.psum_scatter(out[0], "dom", scatter_dimension=0, tiled=True)]
    class_sums, class_weights = finish(pieces, cpg)
    return class_sums, class_weights, out[-1].reshape(count)


def solution(mesh):
    in_specs = (P("dom", "cls"), P("dom", None), P("dom"), P(None, "cls"), P("dom", "cls"), P())
    out_specs = (P("dom", "cls"), P("dom", "cls"), P("dom"))
    return jax.shard_map(local, mesh=mesh, in_specs=in_specs, out_specs=out_specs, check_vma=False)
```

```python
import functools
import math

import jax
import jax.numpy as jnp
from jax import lax
from jax.experimental import pallas as pl
from jax.experimental.pallas import tpu as pltpu
from jax.sharding import PartitionSpec as P

f32, bf16 = jnp.float32, jnp.bfloat16
VMEM = pl.BlockSpec(memory_space=pltpu.VMEM)
SMEM = pl.BlockSpec(memory_space=pltpu.SMEM)
LANES, ROWS = 128, 8
PREPARE = 4_000_000_000
EARLY = 20_000_000_000
NN = (((1,), (0,)), ((), ()))
NT = (((1,), (1,)), ((), ()))


def dot(a, b, dims):
    return lax.dot_general(a, b, dims, preferred_element_type=f32)


def split(x, parts):
    out = []
    for _ in range(parts):
        out.append(x.astype(bf16))
        x = x - out[-1].astype(f32)
    return out


def limits(mib, flops, moved, transcendentals=0):
    return dict(
        compiler_params=pltpu.CompilerParams(vmem_limit_bytes=mib << 20),
        cost_estimate=pl.CostEstimate(flops=flops, bytes_accessed=moved, transcendentals=transcendentals),
    )


def group_at(place, here):
    return place ^ here[0]


def block_spec(steps, shape, dim):
    if steps == 1:
        return VMEM
    index = lambda i: tuple(i if d == dim else 0 for d in range(len(shape)))
    return pl.BlockSpec(shape, index)


def same_spec(steps, shape):
    return VMEM if steps == 1 else pl.BlockSpec(shape, lambda i: (0,) * len(shape))


def turn_matrix(turns, i, pack, inside):
    _, angles, width = turns.shape
    per = LANES // angles
    wide = []
    for j in range(pack):
        turn = turns[i * pack + j]
        turn = jnp.concatenate([jnp.concatenate([turn] * (LANES // width), axis=1)] * per, axis=0)
        wide.append(jnp.where(inside, turn, jnp.zeros((), bf16)))
    return jnp.concatenate(wide, axis=1)


def same_cycle(angles):
    row = lax.broadcasted_iota(jnp.int32, (LANES, LANES), 0) // angles
    col = lax.broadcasted_iota(jnp.int32, (LANES, LANES), 1) // angles
    return row == col


def seed_kernel(out):
    out[...] = lax.broadcasted_iota(jnp.int32, out.shape, 0)


def seed():
    return pl.pallas_call(
        seed_kernel,
        out_specs=VMEM,
        out_shape=jax.ShapeDtypeStruct((LANES, 2 * LANES), jnp.int32),
        name="seed",
        **limits(4, EARLY, 0),
    )()


def start_kernel(numbers, own_in, pixels, turns, table, kind, names_in, weighted, power, names, own, turns2):
    names[...] = names_in[...]
    own[...] = own_in[...]
    for i in range(turns.shape[0]):
        turns2[i] = jnp.concatenate([turns[i]] * (LANES // turns.shape[2]), axis=1)
    kinds, width = table.shape
    power[...] = jnp.concatenate(split(table[...] * table[...], 2), axis=0)
    table3 = jnp.concatenate(split(table[...], 3), axis=0)
    count = pixels.shape[0]
    rows = math.gcd(count, 256)
    ids = numbers[:, :rows]
    for i in range(count // rows):
        at = slice(i * rows, (i + 1) * rows)
        hit = jnp.where((ids % kinds == kind[:, at]) & (ids < 3 * kinds), 1.0, 0.0).T.astype(bf16)
        factor = dot(hit[:, :3 * kinds], table3, NN)
        weighted[at, :width] = (pixels[at, :].astype(f32) * factor).astype(bf16)
        weighted[at, width:] = hit


def start(particles, references, turns, table, kind, names):
    count, pixels = particles.shape
    kinds = table.shape[0]
    return pl.pallas_call(
        start_kernel,
        in_specs=[VMEM] * 7,
        out_specs=[VMEM] * 5,
        out_shape=[
            jax.ShapeDtypeStruct((count, pixels + LANES), bf16),
            jax.ShapeDtypeStruct((2 * kinds, pixels), bf16),
            jax.ShapeDtypeStruct(names.shape, jnp.int32),
            jax.ShapeDtypeStruct(references.shape, bf16),
            jax.ShapeDtypeStruct(turns.shape[:2] + (LANES,), bf16),
        ],
        name="start",
        **limits(16, 1 << 20, 0),
    )(seed(), references, particles, turns, table, kind, names)


def prepare_kernel(pack, after, turns, power, matrix, response, sign):
    sign[...] = jnp.zeros_like(sign)
    turn_count, angles, _ = turns.shape
    kinds, width = power.shape[0] // 2, power.shape[1]
    tiles = width // LANES
    inside = same_cycle(angles)
    lhs = jnp.concatenate(
        [
            jnp.concatenate(
                [power[k * kinds:(k + 1) * kinds, t * LANES:(t + 1) * LANES] for k in range(2)], axis=1
            )
            for t in range(tiles)
        ],
        axis=0,
    )
    for i in range(turn_count // pack):
        wide = turn_matrix(turns, i, pack, inside)
        matrix[i * LANES:(i + 1) * LANES, :] = wide
        value = dot(lhs, jnp.concatenate([wide, wide], axis=0), NN).astype(bf16)
        for j in range(pack):
            for t in range(tiles):
                response[i * kinds:(i + 1) * kinds, j * width + t * LANES:j * width + (t + 1) * LANES] = value[
                    t * kinds:(t + 1) * kinds, j * LANES:(j + 1) * LANES
                ]


def prepare(turns, power, pack, after):
    turn_count = turns.shape[0]
    kinds, pixels = power.shape[0] // 2, power.shape[1]
    steps = turn_count // pack
    return pl.pallas_call(
        functools.partial(prepare_kernel, pack),
        in_specs=[VMEM] * 3,
        out_specs=[VMEM] * 3,
        out_shape=[
            jax.ShapeDtypeStruct((steps * LANES, pack * LANES), bf16),
            jax.ShapeDtypeStruct((steps * kinds, pack * pixels), bf16),
            jax.ShapeDtypeStruct((ROWS, LANES), f32),
        ],
        name="prepare",
        **limits(16, PREPARE, 0),
    )(after, turns, power)


def rotate_kernel(groups, pack, power2, turns, *rest):
    refs = rest[:-4]
    rotated, mean, center, energy = rest[-4:]
    turn_count, angles, _ = turns.shape
    inside_cycle = same_cycle(angles)
    kinds, pixels = power2.shape[0] // 2, power2.shape[1]
    cpg = ROWS // pack
    tiles = pixels // LANES
    group_pairs = cpg * turn_count
    source = jnp.concatenate([block[...].astype(f32) for block in refs], axis=0)
    line = lax.broadcasted_iota(jnp.int32, (ROWS, pixels), 0) // cpg
    copies = []
    for i in range(groups // pack):
        tile = source[i * ROWS:(i + 1) * ROWS, :]
        for k in range(pack):
            out = tile
            for j in range(pack):
                if j != k:
                    out = jnp.where(line == j, pltpu.roll(tile, (j - k) % pack * cpg, 0), out)
            copies.append(out)
    source = jnp.concatenate(copies, axis=0)
    inside = lax.broadcasted_iota(jnp.int32, (groups * ROWS, LANES), 0) % ROWS // cpg
    lhs = jnp.concatenate(
        [
            jnp.concatenate(
                [jnp.where(inside == j, source[:, t * LANES:(t + 1) * LANES], 0.0) for j in range(pack)], axis=1
            )
            for t in range(tiles)
        ],
        axis=0,
    ).astype(bf16)
    for s in range(turn_count // (2 * pack)):
        both = [turn_matrix(turns, 2 * s + h, pack, inside_cycle) for h in range(2)]
        value = dot(lhs, jnp.concatenate(both, axis=0), NT)
        for t in range(tiles):
            for g in range(groups):
                at = (t * groups + g) * ROWS
                pair = [value[at:at + ROWS, h * LANES:(h + 1) * LANES] for h in range(2)]
                to = g * group_pairs + s * 2 * ROWS
                rotated[to:to + 2 * ROWS, t * LANES:(t + 1) * LANES] = jnp.concatenate(pair, axis=0).astype(bf16)
    power = power2[...]
    pairs = groups * group_pairs
    rows = math.gcd(pairs, 256)
    summed = jnp.zeros((kinds, 1), f32)
    for i in range(pairs // rows):
        at = slice(i * rows, (i + 1) * rows)
        value = rotated[at, :pixels].astype(f32)
        hi, lo = split(value * value, 2)
        total = dot(power, hi, NT) + dot(power, lo, NT)
        total = -0.5 * (total[:kinds] + total[kinds:])
        energy[:, at] = total
        summed = summed + jnp.sum(total, axis=1, keepdims=True)

    @pl.when(pl.program_id(0) == 0)
    def _():
        center[...] = summed * (1.0 / pairs)

    spread = lax.broadcasted_iota(jnp.int32, (kinds, LANES), 0) == lax.broadcasted_iota(jnp.int32, (kinds, LANES), 1)
    mean[...] = jnp.sum(jnp.where(spread, center[...], 0.0), axis=0, keepdims=True)
    blank = jnp.zeros((LANES, LANES - 2 * kinds), bf16)
    for i in range(pairs // LANES):
        at = slice(i * LANES, (i + 1) * LANES)
        parts = jnp.concatenate(split(energy[:, at] - center[...], 2), axis=0).T
        rotated[at, pixels:] = jnp.concatenate([parts, blank], axis=1)


def rotate(refs, turns, power2, pack, groups):
    kinds, pixels = power2.shape[0] // 2, power2.shape[1]
    turn_count = turns.shape[0]
    cpg = ROWS // pack
    groups_all = sum(block.shape[0] for block in refs) // cpg
    steps = groups_all // groups
    pairs = groups * cpg * turn_count
    return pl.pallas_call(
        functools.partial(rotate_kernel, groups, pack),
        grid=(steps,),
        in_specs=[same_spec(steps, power2.shape), same_spec(steps, turns.shape)]
        + [block_spec(steps, (block.shape[0] // steps, pixels), 0) for block in refs],
        out_specs=[block_spec(steps, (pairs, pixels + LANES), 0), same_spec(steps, (1, LANES))],
        out_shape=[
            jax.ShapeDtypeStruct((steps * pairs, pixels + LANES), bf16),
            jax.ShapeDtypeStruct((1, LANES), f32),
        ],
        scratch_shapes=[pltpu.VMEM((kinds, 1), f32), pltpu.VMEM((kinds, pairs), f32)],
        name="rotate",
        **limits(12 if steps == 1 else 32, 8 * steps * pairs * pixels * 64, 2 * steps * pairs * pixels),
    )(power2, turns, *refs)


def score_kernel(groups, scale, begin, me, here, weighted, names, rotated, *rest):
    outs, acc = rest[:-1], rest[-1]
    step = pl.program_id(0)
    count = acc.shape[1]
    pairs = rotated.shape[0] // groups
    span = math.gcd(count, 256)
    for n in range(count // span):
        cols = slice(n * span, (n + 1) * span)
        at = slice(begin + n * span, begin + (n + 1) * span)
        pix = weighted[at, :]
        for g in range(groups):
            value = scale * dot(rotated[g * pairs:(g + 1) * pairs, :], pix, NT)
            group = group_at(step * groups + g, here)
            for k in range(2):
                rows = slice(k * pairs, (k + 1) * pairs)
                hit = names[k:k + 1, at] == group
                if g == 0:
                    hit = hit | (step == 0)
                acc[rows, cols] = jnp.where(hit, value, acc[rows, cols])

    @pl.when(step == pl.num_programs(0) - 1)
    def _():
        share = outs[0].shape[1]
        for k, out in enumerate(outs):
            start = pl.multiple_of((me[0] ^ k) * share, share)
            out[...] = acc[:, pl.ds(start, share)]


def score(begin, count, weighted, names, rotated, me, here, peers, group_pairs, groups, scale):
    width = weighted.shape[1]
    steps = rotated.shape[0] // (group_pairs * groups)
    share = count // peers
    rows = 2 * group_pairs
    return pl.pallas_call(
        functools.partial(score_kernel, groups, scale, begin),
        grid=(steps,),
        in_specs=[
            SMEM,
            SMEM,
            same_spec(steps, weighted.shape),
            same_spec(steps, names.shape),
            block_spec(steps, (groups * group_pairs, width), 0),
        ],
        out_specs=[same_spec(steps, (rows, share))] * peers,
        out_shape=[jax.ShapeDtypeStruct((rows, share), f32)] * peers,
        scratch_shapes=[pltpu.VMEM((rows, count), f32)],
        name="score",
        **limits(12 if steps == 1 else 32, 2 * rotated.shape[0] * width * count, 2 * rotated.shape[0] * width),
    )(me, here, weighted, names, rotated)


def soften_kernel(scores, mean, *rest):
    out = rest[-1]
    value = scores[...]
    rows, share = value.shape
    top = jnp.max(value, axis=0, keepdims=True)
    grown = jnp.exp(value - top)
    total = jnp.sum(grown, axis=0, keepdims=True)
    out[:rows, :] = (grown * (1.0 / total)).astype(bf16)
    tail = jnp.zeros((2 * ROWS, share), f32)
    at = lax.broadcasted_iota(jnp.int32, tail.shape, 0)
    centers = mean[...]
    if share > LANES:
        centers = jnp.concatenate([centers, jnp.zeros((1, share - LANES), f32)], axis=1)
    for i, row in enumerate(split(top + jnp.log(total), 3) + split(centers, 3)):
        tail = jnp.where(at == i, row.astype(f32), tail)
    out[rows:, :] = tail.astype(bf16)


def soften(scores, mean, *after):
    rows, share = scores.shape
    return pl.pallas_call(
        soften_kernel,
        in_specs=[VMEM] * (2 + len(after)),
        out_specs=VMEM,
        out_shape=jax.ShapeDtypeStruct((rows + 2 * ROWS, share), bf16),
        name="soften",
        **limits(8, 4 * rows * share, 6 * rows * share, rows * share),
    )(scores, mean, *after)


def collect_kernel(groups, parts, turn_count, kinds, scale, begin, peers, first, last, me, here, names, weighted, *rest):
    rest = list(rest)
    take = lambda n: [rest.pop(0) for _ in range(n)]
    matrix, response = take(2) if last else (None, None)
    blocks = take(peers)
    before = None if first else take(3)
    sums = take(parts) if last else None
    logs, weights, lhs, by_kind = rest if last else [rest[i] for i in (2, 3, 0, 1)]
    step = pl.program_id(0)
    pixels = weighted.shape[1] - LANES
    share = blocks[0].shape[1]
    count = share * peers
    rows = weights.shape[0]
    pairs = rows // 2
    turns = lhs.shape[1] // LANES
    pack = turn_count // turns
    cpg = ROWS // pack
    tiles = pixels // LANES
    own = slice(begin, begin + count)

    @pl.when(step == 0)
    def _():
        center = jnp.zeros((1, share), f32)
        for k, block in enumerate(blocks):
            start = pl.multiple_of((me[0] ^ k) * share, share)
            weights[:, pl.ds(start, share)] = block[:rows, :]
            tail = block[rows:, :].astype(f32)
            logs[0:1, pl.ds(begin + start, share)] = tail[0:1] + tail[1:2] + tail[2:3]
            center = center + (tail[3:4] + tail[4:5] + tail[5:6])
        line = lax.broadcasted_iota(jnp.int32, (2 * ROWS, LANES), 0)
        inside = lax.broadcasted_iota(jnp.int32, (2 * ROWS, LANES), 1) < kinds
        stacked = jnp.zeros((2 * ROWS, LANES), f32)
        for i, part in enumerate(split(center[:, :LANES], 3)):
            stacked = jnp.where((line == i) & inside, part.astype(f32), stacked)
        moved = dot(stacked.astype(bf16), weighted[own, pixels:], NT)
        logs[:, own] = logs[:, own] + scale * jnp.sum(moved, axis=0, keepdims=True)
        if not first:
            logs[:, :begin] = before[2][:, :begin]

    halves = 2 if groups % 4 == 0 else 1
    span = groups // halves
    row_of = lambda t, g: ((g // span * tiles + t) * span + g % span) * ROWS
    totals = []
    zero = jnp.zeros((), bf16)
    for g in range(0, groups, 2):
        dense = []
        for q in range(2):
            group = group_at(step * groups + g + q, here)
            dense.append(
                jnp.where(names[0:1, own] == group, weights[:pairs, :], zero)
                + jnp.where(names[1:2, own] == group, weights[pairs:, :], zero)
            )
        value = dot(jnp.concatenate(dense, axis=0), weighted[own, :], NN)
        for i in range(turns):
            lanes = slice(i * LANES, (i + 1) * LANES)
            for t in range(tiles):
                pair = [
                    value[q * pairs + i * ROWS:q * pairs + (i + 1) * ROWS, t * LANES:(t + 1) * LANES]
                    for q in range(2)
                ]
                pair = jnp.concatenate(pair, axis=0)
                at = slice(row_of(t, g), row_of(t, g) + 2 * ROWS)
                if not first:
                    pair = pair + before[0][at, lanes]
                lhs[at, lanes] = pair.astype(lhs.dtype)
            for q in range(2):
                by_kind[(g + q) * ROWS:(g + q + 1) * ROWS, i * kinds:(i + 1) * kinds] = value[
                    q * pairs + i * ROWS:q * pairs + (i + 1) * ROWS, pixels:pixels + kinds
                ]
        if last and (g + 2) % span == 0:
            at = slice(len(totals) * tiles * span * ROWS, (len(totals) + 1) * tiles * span * ROWS)
            totals.append(dot(lhs[at, :], matrix[...], NN))
    if not last:
        if not first:
            by_kind[...] = by_kind[...] + before[1][...]
        return
    light = by_kind[...] if first else by_kind[...] + before[1][...]
    heavy = dot(jnp.concatenate(split(light, 2), axis=0), response[...], NN)
    heavy = heavy[:groups * ROWS] + heavy[groups * ROWS:]
    upper = lax.broadcasted_iota(jnp.int32, (ROWS, LANES), 0) < cpg

    def fold(terms):
        out = terms[0]
        for j in range(1, pack):
            out = out + pltpu.roll(terms[j], ROWS - j * cpg, 0)
        return out

    for g in range(groups):
        part, to = g % parts, slice(g // parts * ROWS, (g // parts + 1) * ROWS)
        for t in range(tiles):
            lanes = slice(t * LANES, (t + 1) * LANES)
            at = slice((t * span + g % span) * ROWS, (t * span + g % span + 1) * ROWS)
            top = fold([totals[g // span][at, j * LANES:(j + 1) * LANES] for j in range(pack)])
            at = slice(g * ROWS, (g + 1) * ROWS)
            low = fold(
                [heavy[at, j * pixels + t * LANES:j * pixels + (t + 1) * LANES] for j in range(pack)]
            )
            sums[part][to, lanes] = jnp.where(upper, top, pltpu.roll(low, cpg, 0))


def collect(
    begin, blocks, before, last, names, weighted, matrix, response, me, here, parts, turn_count, kinds, group_pairs,
    groups, groups_all, scale
):
    count, width = weighted.shape
    pixels = width - LANES
    peers = len(blocks)
    steps = groups_all // groups
    turns = matrix.shape[0] // LANES
    rows = groups * ROWS // parts
    first = not before
    left = (pixels // LANES * groups * ROWS, turns * LANES)
    light = (groups * ROWS, turns * kinds)
    logs_spec = same_spec(steps, (1, count))
    logs_shape = jax.ShapeDtypeStruct((1, count), f32)
    sides = [block_spec(steps, left, 0), block_spec(steps, light, 0)]
    weights_scratch = pltpu.VMEM((2 * group_pairs, peers * blocks[0].shape[1]), bf16)
    if last:
        out_specs = [block_spec(steps, (rows, pixels), 0)] * parts + [logs_spec]
        out_shape = [jax.ShapeDtypeStruct((steps * rows, pixels), f32)] * parts + [logs_shape]
        scratch = [weights_scratch, pltpu.VMEM(left, bf16), pltpu.VMEM(light, f32)]
    else:
        out_specs = sides + [logs_spec]
        out_shape = [jax.ShapeDtypeStruct((steps * shape[0], shape[1]), f32) for shape in (left, light)] + [logs_shape]
        scratch = [weights_scratch]
    both = [names, weighted] + ([matrix, response] if last else []) + blocks
    return pl.pallas_call(
        functools.partial(
            collect_kernel, groups, parts, turn_count, kinds, scale, begin, peers, first, last
        ),
        grid=(steps,),
        in_specs=[SMEM, SMEM]
        + [same_spec(steps, a.shape) for a in both]
        + ([] if first else sides + [logs_spec]),
        out_specs=out_specs,
        out_shape=out_shape,
        scratch_shapes=scratch,
        name="collect",
        **limits(
            20 if steps == 1 else 56, 2 * groups_all * group_pairs * width * peers * blocks[0].shape[1],
            4 * count * pixels
        ),
    )(me, here, *both, *before)


def add_kernel(left, right, *outs):
    rows = outs[0].shape[0]
    for i, out in enumerate(outs):
        at = slice(i * rows, (i + 1) * rows)
        out[...] = left[at, :] + right[at, :]


def add_cut(left, right, pieces):
    shape = (left.shape[0] // pieces, left.shape[1])
    return pl.pallas_call(
        add_kernel,
        in_specs=[VMEM, VMEM],
        out_specs=[VMEM] * pieces,
        out_shape=[jax.ShapeDtypeStruct(shape, f32)] * pieces,
        name="add_cut",
        **limits(4, left.size, 12 * left.size),
    )(left, right)


def finish_kernel(*refs):
    sums, weights = refs[-2:]
    total = refs[0][...]
    for ref in refs[1:-2]:
        total = total + ref[...]
    sums[...] = total[:sums.shape[0], :].astype(bf16)
    weights[...] = total[sums.shape[0]:, :]


def finish(pieces, cpg):
    shape = (cpg, pieces[0].shape[1])
    return pl.pallas_call(
        finish_kernel,
        in_specs=[VMEM] * len(pieces),
        out_specs=[VMEM] * 2,
        out_shape=[jax.ShapeDtypeStruct(shape, bf16), jax.ShapeDtypeStruct(shape, f32)],
        name="finish",
        **limits(4, pieces[0].size, 12 * pieces[0].size),
    )(*pieces)


def swap(x, axis, k):
    return lax.ppermute(x, axis, [(i, i ^ k) for i in range(lax.axis_size(axis))])


def local(particles, candidates, defocus, ctf_table, references, rotations):
    count, pixels = particles.shape
    peers = lax.axis_size("cls")
    owners = lax.axis_size("dom")
    paired = owners & (owners - 1) == 0 and 4 <= owners <= 8
    turn_count = rotations.shape[0]
    cpg = references.shape[0]
    pack = ROWS // cpg
    group_pairs = cpg * turn_count
    groups = math.gcd(owners, 8)
    kinds = ctf_table.shape[0]
    scale = 4.0 / math.sqrt(pixels * peers)
    me = lax.axis_index("cls").astype(jnp.int32).reshape(1)
    here = (lax.axis_index("dom") if paired else jnp.int32(0)).astype(jnp.int32).reshape(1)
    weighted, power2, names, own_refs, turns2 = start(
        particles, references, rotations, ctf_table, defocus.reshape(1, count), candidates.T
    )
    if paired:
        line = [own_refs] + [swap(references, "dom", 2 * k) for k in range(1, owners // 2)]
        refs = [half for block in line for half in (block, swap(references if block is own_refs else block, "dom", 1))]
    else:
        refs = [lax.all_gather(references, "dom", axis=0, tiled=True)]
    rotated, mean = rotate(refs, turns2, power2, pack, groups)
    chunks = 2
    size = count // chunks
    blocks, signs = [], []
    for c in range(chunks):
        cut = score(c * size, size, weighted, names, rotated, me, here, peers, group_pairs, groups, scale)
        total = cut[0]
        for k in range(1, peers):
            total = total + swap(cut[k].astype(jnp.float16), "cls", k).astype(f32)
        own = soften(total, mean, *signs)
        if c == 0:
            matrix, response, *signs = prepare(turns2, power2, pack, own)
        blocks.append([own] + [swap(own, "cls", k) for k in range(1, peers)])
    parts = 2 if paired else 1
    out = []
    for c in range(chunks):
        out = collect(
            c * size, blocks[c], out, c == chunks - 1, names, weighted, matrix, response, me, here, parts, turn_count,
            kinds, group_pairs, groups, owners, scale
        )
    if paired:
        pieces = add_cut(out[0], swap(out[1], "dom", 1), owners // 2)
        pieces = [pieces[0]] + [swap(pieces[k], "dom", 2 * k) for k in reversed(range(1, owners // 2))]
    else:
        pieces = [lax.psum_scatter(out[0], "dom", scatter_dimension=0, tiled=True)]
    class_sums, class_weights = finish(pieces, cpg)
    return class_sums, class_weights, out[-1].reshape(count)


def solution(mesh):
    in_specs = (P("dom", "cls"), P("dom", None), P("dom"), P(None, "cls"), P("dom", "cls"), P())
    out_specs = (P("dom", "cls"), P("dom", "cls"), P("dom"))
    return jax.shard_map(local, mesh=mesh, in_specs=in_specs, out_specs=out_specs, check_vma=False)
```

```python
import functools
import math

import jax
import jax.numpy as jnp
from jax import lax
from jax.experimental import pallas as pl
from jax.experimental.pallas import tpu as pltpu
from jax.sharding import PartitionSpec as P

f32, bf16 = jnp.float32, jnp.bfloat16
VMEM = pl.BlockSpec(memory_space=pltpu.VMEM)
SMEM = pl.BlockSpec(memory_space=pltpu.SMEM)
LANES, ROWS = 128, 8
PREPARE = 4_000_000_000
EARLY = 20_000_000_000
NN = (((1,), (0,)), ((), ()))
NT = (((1,), (1,)), ((), ()))


def dot(a, b, dims):
    return lax.dot_general(a, b, dims, preferred_element_type=f32)


def split(x, parts):
    out = []
    for _ in range(parts):
        out.append(x.astype(bf16))
        x = x - out[-1].astype(f32)
    return out


def limits(mib, flops, moved, transcendentals=0):
    return dict(
        compiler_params=pltpu.CompilerParams(vmem_limit_bytes=mib << 20),
        cost_estimate=pl.CostEstimate(flops=flops, bytes_accessed=moved, transcendentals=transcendentals),
    )


def group_at(place, here):
    return place ^ here[0]


def block_spec(steps, shape, dim):
    if steps == 1:
        return VMEM
    index = lambda i: tuple(i if d == dim else 0 for d in range(len(shape)))
    return pl.BlockSpec(shape, index)


def same_spec(steps, shape):
    return VMEM if steps == 1 else pl.BlockSpec(shape, lambda i: (0,) * len(shape))


def turn_matrix(turns, i, pack, inside):
    _, angles, width = turns.shape
    per = LANES // angles
    wide = []
    for j in range(pack):
        turn = turns[i * pack + j]
        turn = jnp.concatenate([jnp.concatenate([turn] * (LANES // width), axis=1)] * per, axis=0)
        wide.append(jnp.where(inside, turn, jnp.zeros((), bf16)))
    return jnp.concatenate(wide, axis=1)


def same_cycle(angles):
    row = lax.broadcasted_iota(jnp.int32, (LANES, LANES), 0) // angles
    col = lax.broadcasted_iota(jnp.int32, (LANES, LANES), 1) // angles
    return row == col


def seed_kernel(out):
    out[...] = lax.broadcasted_iota(jnp.int32, out.shape, 0)


def seed():
    return pl.pallas_call(
        seed_kernel,
        out_specs=VMEM,
        out_shape=jax.ShapeDtypeStruct((LANES, 2 * LANES), jnp.int32),
        name="seed",
        **limits(4, EARLY, 0),
    )()


def start_kernel(numbers, own_in, pixels, turns, table, kind, names_in, weighted, power, names, own, turns2):
    names[...] = names_in[...]
    own[...] = own_in[...]
    for i in range(turns.shape[0]):
        turns2[i] = jnp.concatenate([turns[i]] * (LANES // turns.shape[2]), axis=1)
    kinds, width = table.shape
    power[...] = jnp.concatenate(split(table[...] * table[...], 2), axis=0)
    table3 = jnp.concatenate(split(table[...], 3), axis=0)
    count = pixels.shape[0]
    rows = math.gcd(count, 256)
    ids = numbers[:, :rows]
    for i in range(count // rows):
        at = slice(i * rows, (i + 1) * rows)
        hit = jnp.where((ids % kinds == kind[:, at]) & (ids < 3 * kinds), 1.0, 0.0).T.astype(bf16)
        factor = dot(hit[:, :3 * kinds], table3, NN)
        weighted[at, :width] = (pixels[at, :].astype(f32) * factor).astype(bf16)
        weighted[at, width:] = hit


def start(particles, references, turns, table, kind, names):
    count, pixels = particles.shape
    kinds = table.shape[0]
    return pl.pallas_call(
        start_kernel,
        in_specs=[VMEM] * 7,
        out_specs=[VMEM] * 5,
        out_shape=[
            jax.ShapeDtypeStruct((count, pixels + LANES), bf16),
            jax.ShapeDtypeStruct((2 * kinds, pixels), bf16),
            jax.ShapeDtypeStruct(names.shape, jnp.int32),
            jax.ShapeDtypeStruct(references.shape, bf16),
            jax.ShapeDtypeStruct(turns.shape[:2] + (LANES,), bf16),
        ],
        name="start",
        **limits(16, 1 << 20, 0),
    )(seed(), references, particles, turns, table, kind, names)


def prepare_kernel(pack, after, turns, power, matrix, response, sign):
    sign[...] = jnp.zeros_like(sign)
    turn_count, angles, _ = turns.shape
    kinds, width = power.shape[0] // 2, power.shape[1]
    tiles = width // LANES
    inside = same_cycle(angles)
    lhs = jnp.concatenate(
        [
            jnp.concatenate(
                [power[k * kinds:(k + 1) * kinds, t * LANES:(t + 1) * LANES] for k in range(2)], axis=1
            )
            for t in range(tiles)
        ],
        axis=0,
    )
    for i in range(turn_count // pack):
        wide = turn_matrix(turns, i, pack, inside)
        matrix[i * LANES:(i + 1) * LANES, :] = wide
        value = dot(lhs, jnp.concatenate([wide, wide], axis=0), NN).astype(bf16)
        for j in range(pack):
            for t in range(tiles):
                response[i * kinds:(i + 1) * kinds, j * width + t * LANES:j * width + (t + 1) * LANES] = value[
                    t * kinds:(t + 1) * kinds, j * LANES:(j + 1) * LANES
                ]


def prepare(turns, power, pack, after):
    turn_count = turns.shape[0]
    kinds, pixels = power.shape[0] // 2, power.shape[1]
    steps = turn_count // pack
    return pl.pallas_call(
        functools.partial(prepare_kernel, pack),
        in_specs=[VMEM] * 3,
        out_specs=[VMEM] * 3,
        out_shape=[
            jax.ShapeDtypeStruct((steps * LANES, pack * LANES), bf16),
            jax.ShapeDtypeStruct((steps * kinds, pack * pixels), bf16),
            jax.ShapeDtypeStruct((ROWS, LANES), f32),
        ],
        name="prepare",
        **limits(16, PREPARE, 0),
    )(after, turns, power)


def rotate_kernel(groups, pack, power2, turns, *rest):
    refs = rest[:-4]
    rotated, mean, center, energy = rest[-4:]
    turn_count, angles, _ = turns.shape
    inside_cycle = same_cycle(angles)
    kinds, pixels = power2.shape[0] // 2, power2.shape[1]
    cpg = ROWS // pack
    tiles = pixels // LANES
    group_pairs = cpg * turn_count
    source = jnp.concatenate([block[...].astype(f32) for block in refs], axis=0)
    line = lax.broadcasted_iota(jnp.int32, (ROWS, pixels), 0) // cpg
    copies = []
    for i in range(groups // pack):
        tile = source[i * ROWS:(i + 1) * ROWS, :]
        for k in range(pack):
            out = tile
            for j in range(pack):
                if j != k:
                    out = jnp.where(line == j, pltpu.roll(tile, (j - k) % pack * cpg, 0), out)
            copies.append(out)
    source = jnp.concatenate(copies, axis=0)
    inside = lax.broadcasted_iota(jnp.int32, (groups * ROWS, LANES), 0) % ROWS // cpg
    lhs = jnp.concatenate(
        [
            jnp.concatenate(
                [jnp.where(inside == j, source[:, t * LANES:(t + 1) * LANES], 0.0) for j in range(pack)], axis=1
            )
            for t in range(tiles)
        ],
        axis=0,
    ).astype(bf16)
    for s in range(turn_count // (2 * pack)):
        both = [turn_matrix(turns, 2 * s + h, pack, inside_cycle) for h in range(2)]
        value = dot(lhs, jnp.concatenate(both, axis=0), NT)
        for t in range(tiles):
            for g in range(groups):
                at = (t * groups + g) * ROWS
                pair = [value[at:at + ROWS, h * LANES:(h + 1) * LANES] for h in range(2)]
                to = g * group_pairs + s * 2 * ROWS
                rotated[to:to + 2 * ROWS, t * LANES:(t + 1) * LANES] = jnp.concatenate(pair, axis=0).astype(bf16)
    power = power2[...]
    pairs = groups * group_pairs
    rows = math.gcd(pairs, 256)
    summed = jnp.zeros((kinds, 1), f32)
    for i in range(pairs // rows):
        at = slice(i * rows, (i + 1) * rows)
        value = rotated[at, :pixels].astype(f32)
        hi, lo = split(value * value, 2)
        total = dot(power, hi, NT) + dot(power, lo, NT)
        total = -0.5 * (total[:kinds] + total[kinds:])
        energy[:, at] = total
        summed = summed + jnp.sum(total, axis=1, keepdims=True)

    @pl.when(pl.program_id(0) == 0)
    def _():
        center[...] = summed * (1.0 / pairs)

    spread = lax.broadcasted_iota(jnp.int32, (kinds, LANES), 0) == lax.broadcasted_iota(jnp.int32, (kinds, LANES), 1)
    mean[...] = jnp.sum(jnp.where(spread, center[...], 0.0), axis=0, keepdims=True)
    blank = jnp.zeros((LANES, LANES - 2 * kinds), bf16)
    for i in range(pairs // LANES):
        at = slice(i * LANES, (i + 1) * LANES)
        parts = jnp.concatenate(split(energy[:, at] - center[...], 2), axis=0).T
        rotated[at, pixels:] = jnp.concatenate([parts, blank], axis=1)


def rotate(refs, turns, power2, pack, groups):
    kinds, pixels = power2.shape[0] // 2, power2.shape[1]
    turn_count = turns.shape[0]
    cpg = ROWS // pack
    groups_all = sum(block.shape[0] for block in refs) // cpg
    steps = groups_all // groups
    pairs = groups * cpg * turn_count
    return pl.pallas_call(
        functools.partial(rotate_kernel, groups, pack),
        grid=(steps,),
        in_specs=[same_spec(steps, power2.shape), same_spec(steps, turns.shape)]
        + [block_spec(steps, (block.shape[0] // steps, pixels), 0) for block in refs],
        out_specs=[block_spec(steps, (pairs, pixels + LANES), 0), same_spec(steps, (1, LANES))],
        out_shape=[
            jax.ShapeDtypeStruct((steps * pairs, pixels + LANES), bf16),
            jax.ShapeDtypeStruct((1, LANES), f32),
        ],
        scratch_shapes=[pltpu.VMEM((kinds, 1), f32), pltpu.VMEM((kinds, pairs), f32)],
        name="rotate",
        **limits(12 if steps == 1 else 32, 8 * steps * pairs * pixels * 64, 2 * steps * pairs * pixels),
    )(power2, turns, *refs)


def score_kernel(groups, scale, begin, me, here, weighted, names, rotated, *rest):
    outs, acc = rest[:-1], rest[-1]
    step = pl.program_id(0)
    count = acc.shape[1]
    pairs = rotated.shape[0] // groups
    span = math.gcd(count, 256)
    for n in range(count // span):
        cols = slice(n * span, (n + 1) * span)
        at = slice(begin + n * span, begin + (n + 1) * span)
        pix = weighted[at, :]
        for g in range(groups):
            value = scale * dot(rotated[g * pairs:(g + 1) * pairs, :], pix, NT)
            group = group_at(step * groups + g, here)
            for k in range(2):
                rows = slice(k * pairs, (k + 1) * pairs)
                hit = names[k:k + 1, at] == group
                if g == 0:
                    hit = hit | (step == 0)
                acc[rows, cols] = jnp.where(hit, value, acc[rows, cols])

    @pl.when(step == pl.num_programs(0) - 1)
    def _():
        share = outs[0].shape[1]
        for k, out in enumerate(outs):
            start = pl.multiple_of((me[0] ^ k) * share, share)
            out[...] = acc[:, pl.ds(start, share)]


def score(begin, count, weighted, names, rotated, me, here, peers, group_pairs, groups, scale):
    width = weighted.shape[1]
    steps = rotated.shape[0] // (group_pairs * groups)
    share = count // peers
    rows = 2 * group_pairs
    return pl.pallas_call(
        functools.partial(score_kernel, groups, scale, begin),
        grid=(steps,),
        in_specs=[
            SMEM,
            SMEM,
            same_spec(steps, weighted.shape),
            same_spec(steps, names.shape),
            block_spec(steps, (groups * group_pairs, width), 0),
        ],
        out_specs=[same_spec(steps, (rows, share))] * peers,
        out_shape=[jax.ShapeDtypeStruct((rows, share), f32)] * peers,
        scratch_shapes=[pltpu.VMEM((rows, count), f32)],
        name="score",
        **limits(12 if steps == 1 else 32, 2 * rotated.shape[0] * width * count, 2 * rotated.shape[0] * width),
    )(me, here, weighted, names, rotated)


def soften_kernel(scores, mean, *rest):
    out = rest[-1]
    value = scores[...]
    rows, share = value.shape
    top = jnp.max(value, axis=0, keepdims=True)
    grown = jnp.exp(value - top)
    total = jnp.sum(grown, axis=0, keepdims=True)
    out[:rows, :] = (grown * (1.0 / total)).astype(bf16)
    tail = jnp.zeros((2 * ROWS, share), f32)
    at = lax.broadcasted_iota(jnp.int32, tail.shape, 0)
    centers = mean[...]
    if share > LANES:
        centers = jnp.concatenate([centers, jnp.zeros((1, share - LANES), f32)], axis=1)
    for i, row in enumerate(split(top + jnp.log(total), 3) + split(centers, 3)):
        tail = jnp.where(at == i, row.astype(f32), tail)
    out[rows:, :] = tail.astype(bf16)


def soften(scores, mean, *after):
    rows, share = scores.shape
    return pl.pallas_call(
        soften_kernel,
        in_specs=[VMEM] * (2 + len(after)),
        out_specs=VMEM,
        out_shape=jax.ShapeDtypeStruct((rows + 2 * ROWS, share), bf16),
        name="soften",
        **limits(8, 4 * rows * share, 6 * rows * share, rows * share),
    )(scores, mean, *after)


def collect_kernel(groups, parts, turn_count, kinds, scale, begin, peers, first, last, me, here, names, weighted, *rest):
    rest = list(rest)
    take = lambda n: [rest.pop(0) for _ in range(n)]
    matrix, response = take(2) if last else (None, None)
    blocks = take(peers)
    before = None if first else take(3)
    sums = take(parts) if last else None
    logs, weights, lhs, by_kind = rest if last else [rest[i] for i in (2, 3, 0, 1)]
    step = pl.program_id(0)
    pixels = weighted.shape[1] - LANES
    share = blocks[0].shape[1]
    count = share * peers
    rows = weights.shape[0]
    pairs = rows // 2
    turns = lhs.shape[1] // LANES
    pack = turn_count // turns
    cpg = ROWS // pack
    tiles = pixels // LANES
    own = slice(begin, begin + count)

    @pl.when(step == 0)
    def _():
        center = jnp.zeros((1, share), f32)
        for k, block in enumerate(blocks):
            start = pl.multiple_of((me[0] ^ k) * share, share)
            weights[:, pl.ds(start, share)] = block[:rows, :]
            tail = block[rows:, :].astype(f32)
            logs[0:1, pl.ds(begin + start, share)] = tail[0:1] + tail[1:2] + tail[2:3]
            center = center + (tail[3:4] + tail[4:5] + tail[5:6])
        line = lax.broadcasted_iota(jnp.int32, (2 * ROWS, LANES), 0)
        inside = lax.broadcasted_iota(jnp.int32, (2 * ROWS, LANES), 1) < kinds
        stacked = jnp.zeros((2 * ROWS, LANES), f32)
        for i, part in enumerate(split(center[:, :LANES], 3)):
            stacked = jnp.where((line == i) & inside, part.astype(f32), stacked)
        moved = dot(stacked.astype(bf16), weighted[own, pixels:], NT)
        logs[:, own] = logs[:, own] + scale * jnp.sum(moved, axis=0, keepdims=True)
        if not first:
            logs[:, :begin] = before[2][:, :begin]

    halves = 2 if groups % 4 == 0 else 1
    span = groups // halves
    row_of = lambda t, g: ((g // span * tiles + t) * span + g % span) * ROWS
    totals = []
    zero = jnp.zeros((), bf16)
    for g in range(0, groups, 2):
        dense = []
        for q in range(2):
            group = group_at(step * groups + g + q, here)
            dense.append(
                jnp.where(names[0:1, own] == group, weights[:pairs, :], zero)
                + jnp.where(names[1:2, own] == group, weights[pairs:, :], zero)
            )
        value = dot(jnp.concatenate(dense, axis=0), weighted[own, :], NN)
        for i in range(turns):
            lanes = slice(i * LANES, (i + 1) * LANES)
            for t in range(tiles):
                pair = [
                    value[q * pairs + i * ROWS:q * pairs + (i + 1) * ROWS, t * LANES:(t + 1) * LANES]
                    for q in range(2)
                ]
                pair = jnp.concatenate(pair, axis=0)
                at = slice(row_of(t, g), row_of(t, g) + 2 * ROWS)
                if not first:
                    pair = pair + before[0][at, lanes]
                lhs[at, lanes] = pair.astype(lhs.dtype)
            for q in range(2):
                by_kind[(g + q) * ROWS:(g + q + 1) * ROWS, i * kinds:(i + 1) * kinds] = value[
                    q * pairs + i * ROWS:q * pairs + (i + 1) * ROWS, pixels:pixels + kinds
                ]
        if last and (g + 2) % span == 0:
            at = slice(len(totals) * tiles * span * ROWS, (len(totals) + 1) * tiles * span * ROWS)
            totals.append(dot(lhs[at, :], matrix[...], NN))
    if not last:
        if not first:
            by_kind[...] = by_kind[...] + before[1][...]
        return
    light = by_kind[...] if first else by_kind[...] + before[1][...]
    heavy = dot(jnp.concatenate(split(light, 2), axis=0), response[...], NN)
    heavy = heavy[:groups * ROWS] + heavy[groups * ROWS:]
    upper = lax.broadcasted_iota(jnp.int32, (ROWS, LANES), 0) < cpg

    def fold(terms):
        out = terms[0]
        for j in range(1, pack):
            out = out + pltpu.roll(terms[j], ROWS - j * cpg, 0)
        return out

    for g in range(groups):
        part, to = g % parts, slice(g // parts * ROWS, (g // parts + 1) * ROWS)
        for t in range(tiles):
            lanes = slice(t * LANES, (t + 1) * LANES)
            at = slice((t * span + g % span) * ROWS, (t * span + g % span + 1) * ROWS)
            top = fold([totals[g // span][at, j * LANES:(j + 1) * LANES] for j in range(pack)])
            at = slice(g * ROWS, (g + 1) * ROWS)
            low = fold(
                [heavy[at, j * pixels + t * LANES:j * pixels + (t + 1) * LANES] for j in range(pack)]
            )
            sums[part][to, lanes] = jnp.where(upper, top, pltpu.roll(low, cpg, 0))


def collect(
    begin, blocks, before, last, names, weighted, matrix, response, me, here, parts, turn_count, kinds, group_pairs,
    groups, groups_all, scale
):
    count, width = weighted.shape
    pixels = width - LANES
    peers = len(blocks)
    steps = groups_all // groups
    turns = matrix.shape[0] // LANES
    rows = groups * ROWS // parts
    first = not before
    left = (pixels // LANES * groups * ROWS, turns * LANES)
    light = (groups * ROWS, turns * kinds)
    logs_spec = same_spec(steps, (1, count))
    logs_shape = jax.ShapeDtypeStruct((1, count), f32)
    sides = [block_spec(steps, left, 0), block_spec(steps, light, 0)]
    weights_scratch = pltpu.VMEM((2 * group_pairs, peers * blocks[0].shape[1]), bf16)
    if last:
        out_specs = [block_spec(steps, (rows, pixels), 0)] * parts + [logs_spec]
        out_shape = [jax.ShapeDtypeStruct((steps * rows, pixels), f32)] * parts + [logs_shape]
        scratch = [weights_scratch, pltpu.VMEM(left, bf16), pltpu.VMEM(light, f32)]
    else:
        out_specs = sides + [logs_spec]
        out_shape = [jax.ShapeDtypeStruct((steps * shape[0], shape[1]), f32) for shape in (left, light)] + [logs_shape]
        scratch = [weights_scratch]
    both = [names, weighted] + ([matrix, response] if last else []) + blocks
    return pl.pallas_call(
        functools.partial(
            collect_kernel, groups, parts, turn_count, kinds, scale, begin, peers, first, last
        ),
        grid=(steps,),
        in_specs=[SMEM, SMEM]
        + [same_spec(steps, a.shape) for a in both]
        + ([] if first else sides + [logs_spec]),
        out_specs=out_specs,
        out_shape=out_shape,
        scratch_shapes=scratch,
        name="collect",
        **limits(
            20 if steps == 1 else 56, 2 * groups_all * group_pairs * width * peers * blocks[0].shape[1],
            4 * count * pixels
        ),
    )(me, here, *both, *before)


def add_kernel(left, right, *outs):
    rows = outs[0].shape[0]
    for i, out in enumerate(outs):
        at = slice(i * rows, (i + 1) * rows)
        out[...] = left[at, :] + right[at, :]


def add_cut(left, right, pieces):
    shape = (left.shape[0] // pieces, left.shape[1])
    return pl.pallas_call(
        add_kernel,
        in_specs=[VMEM, VMEM],
        out_specs=[VMEM] * pieces,
        out_shape=[jax.ShapeDtypeStruct(shape, f32)] * pieces,
        name="add_cut",
        **limits(4, left.size, 12 * left.size),
    )(left, right)


def finish_kernel(*refs):
    sums, weights = refs[-2:]
    total = refs[0][...]
    for ref in refs[1:-2]:
        total = total + ref[...]
    sums[...] = total[:sums.shape[0], :].astype(bf16)
    weights[...] = total[sums.shape[0]:, :]


def finish(pieces, cpg):
    shape = (cpg, pieces[0].shape[1])
    return pl.pallas_call(
        finish_kernel,
        in_specs=[VMEM] * len(pieces),
        out_specs=[VMEM] * 2,
        out_shape=[jax.ShapeDtypeStruct(shape, bf16), jax.ShapeDtypeStruct(shape, f32)],
        name="finish",
        **limits(4, pieces[0].size, 12 * pieces[0].size),
    )(*pieces)


def swap(x, axis, k):
    return lax.ppermute(x, axis, [(i, i ^ k) for i in range(lax.axis_size(axis))])


def local(particles, candidates, defocus, ctf_table, references, rotations):
    count, pixels = particles.shape
    peers = lax.axis_size("cls")
    owners = lax.axis_size("dom")
    paired = owners & (owners - 1) == 0 and 4 <= owners <= 8
    turn_count = rotations.shape[0]
    cpg = references.shape[0]
    pack = ROWS // cpg
    group_pairs = cpg * turn_count
    groups = math.gcd(owners, 8)
    kinds = ctf_table.shape[0]
    scale = 4.0 / math.sqrt(pixels * peers)
    me = lax.axis_index("cls").astype(jnp.int32).reshape(1)
    here = (lax.axis_index("dom") if paired else jnp.int32(0)).astype(jnp.int32).reshape(1)
    weighted, power2, names, own_refs, turns2 = start(
        particles, references, rotations, ctf_table, defocus.reshape(1, count), candidates.T
    )
    if paired:
        line = [own_refs] + [swap(references, "dom", 2 * k) for k in range(1, owners // 2)]
        refs = [half for block in line for half in (block, swap(references if block is own_refs else block, "dom", 1))]
    else:
        refs = [lax.all_gather(references, "dom", axis=0, tiled=True)]
    rotated, mean = rotate(refs, turns2, power2, pack, groups)
    chunks = 2
    size = count // chunks
    blocks, signs = [], []
    for c in range(chunks):
        cut = score(c * size, size, weighted, names, rotated, me, here, peers, group_pairs, groups, scale)
        total = cut[0]
        for k in range(1, peers):
            total = total + swap(cut[k].astype(jnp.float16), "cls", k).astype(f32)
        own = soften(total, mean, *signs)
        if c == 0:
            matrix, response, *signs = prepare(turns2, power2, pack, own)
        blocks.append([own] + [swap(own, "cls", k) for k in range(1, peers)])
    parts = 2 if paired else 1
    out = []
    for c in range(chunks):
        out = collect(
            c * size, blocks[c], out, c == chunks - 1, names, weighted, matrix, response, me, here, parts, turn_count,
            kinds, group_pairs, groups, owners, scale
        )
    if paired:
        pieces = add_cut(out[0], swap(out[1], "dom", 1), owners // 2)
        pieces = [pieces[0]] + [swap(pieces[k], "dom", 2 * k) for k in [owners // 2 - 1, *range(1, owners // 2 - 1)]]
    else:
        pieces = [lax.psum_scatter(out[0], "dom", scatter_dimension=0, tiled=True)]
    class_sums, class_weights = finish(pieces, cpg)
    return class_sums, class_weights, out[-1].reshape(count)


def solution(mesh):
    in_specs = (P("dom", "cls"), P("dom", None), P("dom"), P(None, "cls"), P("dom", "cls"), P())
    out_specs = (P("dom", "cls"), P("dom", "cls"), P("dom"))
    return jax.shard_map(local, mesh=mesh, in_specs=in_specs, out_specs=out_specs, check_vma=False)
```
